32 devices in a mesh: layer: 8 (over y, x, core), lat: 4 (over z).
Axes of the slice: x: 2, y: 2, z: 4, core: 2. Of those that a mesh axis runs over, the one named last changes fastest.
Arguments:
- source: float32 [8, 2, 1536, 128], P('layer', None, 'lat'), may hold values from -6 to 6
- wavenumber: float32 [8, 1536, 128], P('layer', 'lat'), may hold values from 0.1 to 1
- green_down: bfloat16 [8, 2, 1536, 3072], P('layer', None, 'lat'), may hold values from -0.109375 to 0.109375
- green_up: bfloat16 [8, 2, 1536, 3072], P('layer', None, 'lat'), may hold values from -0.109375 to 0.109375
Outputs:
- down_trace: float32 [8, 2, 1536, 128], P('layer', None, 'lat')
- up_trace: float32 [8, 2, 1536, 128], P('layer', None, 'lat')
The draws below stay inside these ranges and needn't reach their ends.
All inputs are finite; a program needn't handle non-finite values.
Results may differ from the reference program's by a relative error of at most 0.017.
Values may be sent and summed in bfloat16 or wider, within the bound.
A program may use at most 64 MiB of HBM per device.

```python
import math
import jax
import jax.numpy as jnp
from jax import lax

WIDTH = 1536
ROWS = 128
RELAX = 4
LAYERS = 8


def levels(rng, dims, pieces, low, largest):
    def one(position, blocks):
        draws = jax.random.uniform(jax.random.fold_in(jax.random.fold_in(rng, 6), position), (blocks,), jnp.float32, low / len(pieces), largest / len(pieces))
        return jnp.repeat(jnp.exp(draws), dims[position] // blocks).reshape((-1,) + (1,) * (len(dims) - position - 1))

    factor_of = one(*pieces[0])
    for cut in pieces[1:]:
        factor_of = factor_of * one(*cut)
    return factor_of


def gaussian(rng, shape, width, bound, cuts=(), held_as=jnp.bfloat16):
    values = width * jax.random.normal(rng, shape, jnp.float32)
    if cuts:
        values = values * levels(rng, shape, cuts, -0.22, 0.18)
    return jnp.clip(values, -bound, bound).astype(held_as)


def setup_inputs(seed: int = 0) -> dict:
    key_list = jax.random.split(jax.random.key(seed), 5)
    source = gaussian(key_list[0], (LAYERS, 2, WIDTH, ROWS), 1.0, 6.0, ((0, 8), (2, 4)), jnp.float32)
    wavenumber = jnp.clip(jnp.exp(math.log(1.0) - 2.3025851 * jax.random.uniform(key_list[1], (LAYERS, WIDTH, ROWS), jnp.float32) ** levels(key_list[1], (LAYERS, WIDTH, ROWS), ((0, 8), (1, 4)), -0.2, 0.2)), 0.1, 1.0)
    green_down = gaussian(key_list[2], (LAYERS, 2, WIDTH, 2 * WIDTH), (2 * WIDTH) ** -0.5, 0.109375, ((0, 8), (2, 4)))
    green_up = gaussian(key_list[3], (LAYERS, 2, WIDTH, 2 * WIDTH), (2 * WIDTH) ** -0.5, 0.109375, ((0, 8), (2, 4)))
    return dict(source=source, wavenumber=wavenumber, green_down=green_down, green_up=green_up)


relax_weight = 0.8
damping = 0.5


def relax_step(field, lateral_pad, forcing, diag_real, diag_imag, inverse_real, inverse_imag):
    along = jnp.pad(field, ((0, 0), (0, 0), (1, 1)))
    beside = lateral_pad[:, 2:] + lateral_pad[:, :-2] + along[:, :, 2:] + along[:, :, :-2]
    apply_real = diag_real * field[0] - diag_imag * field[1] - beside[0]
    apply_imag = diag_real * field[1] + diag_imag * field[0] - beside[1]
    res_real = forcing[0] - apply_real
    res_imag = forcing[1] - apply_imag
    step_real = res_real * inverse_real - res_imag * inverse_imag
    step_imag = res_real * inverse_imag + res_imag * inverse_real
    return field + relax_weight * jnp.stack([step_real, step_imag], 0)


def relax(forcing, wave_sq):
    diag_real = 4.0 - wave_sq
    diag_imag = damping * wave_sq
    denom = diag_real * diag_real + diag_imag * diag_imag
    inverse_real = diag_real / denom
    inverse_imag = -diag_imag / denom
    field = jnp.zeros_like(forcing)
    for sweep in range(RELAX):
        padded = jnp.pad(field, ((0, 0), (1, 1), (0, 0)))
        field = relax_step(field, padded, forcing, diag_real, diag_imag, inverse_real, inverse_imag)
    return field


def sweep_chain(traces, green, backward):
    def turn(carry, pair):
        trace_now, block = pair
        flat = block.reshape(2 * WIDTH, 2 * WIDTH)
        incoming = carry.astype(jnp.bfloat16).reshape(2 * WIDTH, ROWS)
        product = jnp.dot(flat, incoming, preferred_element_type=jnp.float32)
        result = trace_now + product.reshape(2, WIDTH, ROWS)
        return result, result

    start = jnp.zeros((2, WIDTH, ROWS), jnp.float32)
    final, results = lax.scan(turn, start, (traces, green), reverse=backward)
    return results


def reference(source, wavenumber, green_down, green_up):
    traces = jax.vmap(relax)(source, wavenumber)
    down_trace = sweep_chain(traces, green_down, False)
    up_trace = sweep_chain(traces, green_up, True)
    return down_trace, up_trace
```

```python
import functools

import jax
import jax.numpy as jnp
from jax import lax
from jax.experimental import pallas as pl
from jax.experimental.pallas import tpu as pltpu
from jax.sharding import PartitionSpec as P

RELAX = 4
HALO = 8
MESH = pl.DeviceIdType.MESH

relax_weight = 0.8
damping = 0.5


def relaxed(source, wave_sq, inside):
    rows, lanes = wave_sq.shape
    lane = lax.broadcasted_iota(jnp.int32, (rows, lanes), 1)
    first, last = lane == 0, lane == lanes - 1
    diag_real = 4.0 - wave_sq
    diag_imag = damping * wave_sq
    scale = jnp.where(inside, relax_weight, 0.0) / (diag_real * diag_real + diag_imag * diag_imag)
    inverse_real = diag_real * scale
    inverse_imag = -diag_imag * scale

    def beside(field):
        total = pltpu.roll(field, 1, 0) + pltpu.roll(field, rows - 1, 0)
        total = total + jnp.where(first, 0.0, pltpu.roll(field, 1, 1))
        return total + jnp.where(last, 0.0, pltpu.roll(field, lanes - 1, 1))

    real = source[0] * inverse_real - source[1] * inverse_imag
    imag = source[0] * inverse_imag + source[1] * inverse_real
    for _ in range(RELAX - 1):
        res_real = source[0] - (diag_real * real - diag_imag * imag - beside(real))
        res_imag = source[1] - (diag_real * imag + diag_imag * real - beside(imag))
        real = real + res_real * inverse_real - res_imag * inverse_imag
        imag = imag + res_real * inverse_imag + res_imag * inverse_real
    return real, imag


def kernel(layers, slabs, source, wave, green_down, green_up, down, up, green, held, ready, trace, wide_source,
           wide_wave, green_sem, halo_send, halo_recv, send_sem, recv_sem):
    me_layer, me_slab = lax.axis_index("layer"), lax.axis_index("lat")
    slab = trace.shape[1]
    half = slab * slabs // 2

    loads = [
        pltpu.make_async_copy(block, green.at[way], green_sem.at[way])
        for way, block in enumerate((green_down, green_up))
    ]
    for load in loads:
        load.start()

    barrier = pltpu.get_barrier_semaphore()
    me = me_layer * slabs + me_slab

    def greet(other, carry):
        @pl.when(other != me)
        def _():
            pl.semaphore_signal(barrier, inc=1, device_id=(other // slabs, other % slabs), device_id_type=MESH)

        return carry

    lax.fori_loop(0, layers * slabs, greet, 0)
    wide_source[:, HALO : HALO + slab] = source[...]
    wide_wave[HALO : HALO + slab] = wave[...]
    pl.semaphore_wait(barrier, layers * slabs - 1)

    def halo_copies(side):
        rows = pl.ds(slab - HALO, HALO) if side == 0 else pl.ds(0, HALO)
        lands = pl.ds(0, HALO) if side == 0 else pl.ds(HALO + slab, HALO)
        other = me_slab + 1 if side == 0 else me_slab - 1
        other = jnp.clip(other, 0, slabs - 1)
        return [
            pltpu.make_async_remote_copy(
                src_ref=src, dst_ref=dst, send_sem=halo_send.at[side, n], recv_sem=halo_recv.at[side, n],
                device_id=(me_layer, other), device_id_type=MESH,
            )
            for n, (src, dst) in enumerate(
                ((source.at[:, rows], wide_source.at[:, lands]), (wave.at[rows], wide_wave.at[lands]))
            )
        ]

    has_next, has_previous = me_slab < slabs - 1, me_slab > 0
    sends, receives = (has_next, has_previous), (has_previous, has_next)
    for side in range(2):
        @pl.when(sends[side])
        def _():
            for copy in halo_copies(side):
                copy.start()

        @pl.when(jnp.logical_not(receives[side]))
        def _():
            lands = pl.ds(0, HALO) if side == 0 else pl.ds(HALO + slab, HALO)
            wide_source[:, lands] = jnp.zeros((2, HALO, source.shape[2]), jnp.float32)
            wide_wave[lands] = jnp.ones((HALO, source.shape[2]), jnp.float32)

    for side in range(2):
        @pl.when(receives[side])
        def _():
            for copy in halo_copies(side):
                copy.wait_recv()

    row = lax.broadcasted_iota(jnp.int32, wide_wave.shape, 0) - HALO + me_slab * slab
    inside = jnp.logical_and(row >= 0, row < slab * slabs)
    field = relaxed(wide_source[...], wide_wave[...], inside)
    for part in range(2):
        trace[part] = field[part][HALO : HALO + slab]

    def turn_copy(way, target, slot, semaphore):
        here = pl.ds(pl.multiple_of(slot * slab, 16), slab)
        step = jnp.where(way == 0, 1, -1)
        return pltpu.make_async_remote_copy(
            src_ref=ready.at[way], dst_ref=held.at[way, :, here, :],
            send_sem=send_sem.at[way, semaphore], recv_sem=recv_sem.at[way, slot],
            device_id=(jnp.clip(me_layer + step, 0, layers - 1), target), device_id_type=MESH,
        )

    def put(way, part, value):
        ready[way, part] = value.astype(jnp.bfloat16)

        @pl.when(way == 0)
        def _():
            down[part] = value

        @pl.when(way == 1)
        def _():
            up[part] = value

    def turn(order, carry):
        way = jnp.where(me_layer < layers // 2, order, 1 - order)
        place = jnp.where(way == 0, me_layer, layers - 1 - me_layer)

        @pl.when(place == 0)
        def _():
            for part in range(2):
                put(way, part, trace[part])

        @pl.when(place > 0)
        def _():
            pltpu.make_async_copy(green_down, green.at[way], green_sem.at[way]).wait()
            near = me_slab // (slabs // 2)
            totals = [trace[0], trace[1]]
            for turn_half in range(2):
                now = near if turn_half == 0 else 1 - near
                for n in range(slabs // 2):
                    turn_copy(way, me_slab, now * (slabs // 2) + n, 0).wait_recv()
                for part in range(2):
                    for cut in range(2):
                        columns = pl.ds(pl.multiple_of(cut * 2 * half + now * half, 128), half)
                        totals[part] = totals[part] + jnp.dot(
                            green[way, pl.ds(part * slab, slab), columns],
                            held[way, cut, pl.ds(pl.multiple_of(now * half, 16), half), :],
                            preferred_element_type=jnp.float32,
                        )
            for part in range(2):
                put(way, part, totals[part])

        @pl.when(place < layers - 1)
        def _():
            for target in range(slabs):
                turn_copy(way, target, me_slab, target).start()

        return carry

    lax.fori_loop(0, 2, turn, 0)

    for way in range(2):
        place = me_layer if way == 0 else layers - 1 - me_layer

        @pl.when(place == 0)
        def _():
            loads[way].wait()

        @pl.when(place < layers - 1)
        def _():
            for target in range(slabs):
                turn_copy(way, target, me_slab, target).wait_send()

    for side in range(2):
        @pl.when(sends[side])
        def _():
            for copy in halo_copies(side):
                copy.wait_send()


def local(source, wavenumber, green_down, green_up):
    layers, slabs = lax.axis_size("layer"), lax.axis_size("lat")
    _, parts, slab, lanes = source.shape
    width = slab * slabs
    shape = jax.ShapeDtypeStruct((parts, slab, lanes), jnp.float32)
    vmem = pl.BlockSpec(memory_space=pltpu.VMEM)
    anywhere = pl.BlockSpec(memory_space=pl.ANY)
    down, up = pl.pallas_call(
        functools.partial(kernel, layers, slabs),
        out_shape=(shape, shape),
        in_specs=[vmem, vmem, anywhere, anywhere],
        out_specs=(vmem, vmem),
        scratch_shapes=[
            pltpu.VMEM((2, parts * slab, parts * width), jnp.bfloat16),
            pltpu.VMEM((2, parts, width, lanes), jnp.bfloat16),
            pltpu.VMEM((2, parts, slab, lanes), jnp.bfloat16),
            pltpu.VMEM((parts, slab, lanes), jnp.float32),
            pltpu.VMEM((parts, slab + 2 * HALO, lanes), jnp.float32),
            pltpu.VMEM((slab + 2 * HALO, lanes), jnp.float32),
            pltpu.SemaphoreType.DMA((2,)),
            pltpu.SemaphoreType.DMA((2, 2)),
            pltpu.SemaphoreType.DMA((2, 2)),
            pltpu.SemaphoreType.DMA((2, slabs)),
            pltpu.SemaphoreType.DMA((2, slabs)),
        ],
        compiler_params=pltpu.CompilerParams(
            collective_id=0, has_side_effects=True, vmem_limit_bytes=32 * 1024 * 1024
        ),
    )(
        source[0],
        wavenumber[0],
        green_down.reshape(parts * slab, parts * width),
        green_up.reshape(parts * slab, parts * width),
    )
    return down[None], up[None]


def solution(mesh):
    return jax.shard_map(
        local,
        mesh=mesh,
        in_specs=(
            P("layer", None, "lat", None),
            P("layer", "lat", None),
            P("layer", None, "lat", None),
            P("layer", None, "lat", None),
        ),
        out_specs=(P("layer", None, "lat", None), P("layer", None, "lat", None)),
        check_vma=False,
    )
```

```python
import functools

import jax
import jax.numpy as jnp
from jax import lax
from jax.experimental import pallas as pl
from jax.experimental.pallas import tpu as pltpu
from jax.sharding import PartitionSpec as P

RELAX = 4
HALO = 8
MESH = pl.DeviceIdType.MESH

relax_weight = 0.8
damping = 0.5


def relaxed(source, wave_sq, inside):
    rows, lanes = wave_sq.shape
    lane = lax.broadcasted_iota(jnp.int32, (rows, lanes), 1)
    first, last = lane == 0, lane == lanes - 1
    diag_real = 4.0 - wave_sq
    diag_imag = damping * wave_sq
    scale = jnp.where(inside, relax_weight, 0.0) / (diag_real * diag_real + diag_imag * diag_imag)
    inverse_real = diag_real * scale
    inverse_imag = -diag_imag * scale

    def beside(field):
        total = pltpu.roll(field, 1, 0) + pltpu.roll(field, rows - 1, 0)
        total = total + jnp.where(first, 0.0, pltpu.roll(field, 1, 1))
        return total + jnp.where(last, 0.0, pltpu.roll(field, lanes - 1, 1))

    real = source[0] * inverse_real - source[1] * inverse_imag
    imag = source[0] * inverse_imag + source[1] * inverse_real
    for _ in range(RELAX - 1):
        res_real = source[0] - (diag_real * real - diag_imag * imag - beside(real))
        res_imag = source[1] - (diag_real * imag + diag_imag * real - beside(imag))
        real = real + res_real * inverse_real - res_imag * inverse_imag
        imag = imag + res_real * inverse_imag + res_imag * inverse_real
    return real, imag


def kernel(layers, slabs, source, wave, green_down, green_up, down, up, green, held, ready, passing, trace, wide_source,
           wide_wave, load_sem, halo_send, halo_recv, own_send, own_recv, near_send, near_recv, spread_send,
           far_send, far_recv, pass_send, pass_recv):
    me_layer, me_slab = lax.axis_index("layer"), lax.axis_index("lat")
    slab = trace.shape[1]
    half = slab * slabs // 2
    detour = passing.shape[3]
    straight = slab - detour
    middle = pl.ds(HALO, slab)

    loads = [
        pltpu.make_async_copy(src, dst, load_sem.at[n])
        for n, (src, dst) in enumerate(
            (
                (green_down, green.at[0]),
                (green_up, green.at[1]),
                (source, wide_source.at[:, middle]),
                (wave, wide_wave.at[middle]),
            )
        )
    ]
    for n in (2, 3, 0, 1):
        loads[n].start()

    barrier = pltpu.get_barrier_semaphore()
    me = me_layer * slabs + me_slab

    def greet(other, carry):
        @pl.when(other != me)
        def _():
            pl.semaphore_signal(barrier, inc=1, device_id=(other // slabs, other % slabs), device_id_type=MESH)

        return carry

    lax.fori_loop(0, layers * slabs, greet, 0)
    pl.semaphore_wait(barrier, layers * slabs - 1)

    def halo_copies(side):
        rows = pl.ds(slab - HALO, HALO) if side == 0 else pl.ds(0, HALO)
        lands = pl.ds(0, HALO) if side == 0 else pl.ds(HALO + slab, HALO)
        other = me_slab + 1 if side == 0 else me_slab - 1
        other = jnp.clip(other, 0, slabs - 1)
        return [
            pltpu.make_async_remote_copy(
                src_ref=src, dst_ref=dst, send_sem=halo_send.at[side, n], recv_sem=halo_recv.at[side, n],
                device_id=(me_layer, other), device_id_type=MESH,
            )
            for n, (src, dst) in enumerate(
                ((source.at[:, rows], wide_source.at[:, lands]), (wave.at[rows], wide_wave.at[lands]))
            )
        ]

    has_next, has_previous = me_slab < slabs - 1, me_slab > 0
    sends, receives = (has_next, has_previous), (has_previous, has_next)
    for side in range(2):
        @pl.when(sends[side])
        def _():
            for copy in halo_copies(side):
                copy.start()

        @pl.when(jnp.logical_not(receives[side]))
        def _():
            lands = pl.ds(0, HALO) if side == 0 else pl.ds(HALO + slab, HALO)
            wide_source[:, lands] = jnp.zeros((2, HALO, source.shape[2]), jnp.float32)
            wide_wave[lands] = jnp.ones((HALO, source.shape[2]), jnp.float32)

    for n in (2, 3):
        loads[n].wait()
    for side in range(2):
        @pl.when(receives[side])
        def _():
            for copy in halo_copies(side):
                copy.wait_recv()

    row = lax.broadcasted_iota(jnp.int32, wide_wave.shape, 0) - HALO + me_slab * slab
    inside = jnp.logical_and(row >= 0, row < slab * slabs)
    field = relaxed(wide_source[...], wide_wave[...], inside)
    for part in range(2):
        trace[part] = field[part][HALO : HALO + slab]

    def remote(src, dst, send, recv, layer, target):
        return pltpu.make_async_remote_copy(
            src_ref=src, dst_ref=dst, send_sem=send, recv_sem=recv,
            device_id=(jnp.clip(layer, 0, layers - 1), target), device_id_type=MESH,
        )

    def rows_of(slot, begin, count):
        return pl.ds(pl.multiple_of(slot * slab + begin, 16), count)

    def own_copy(way, part, layer):
        here = rows_of(me_slab, 0, slab)
        return remote(ready.at[way, part], held.at[way, part, here, :], own_send.at[way, part],
                      own_recv.at[way, part], layer, me_slab)

    def near_copy(way, part, layer, target, slot):
        here = rows_of(slot, 0, straight)
        return remote(ready.at[way, part, pl.ds(0, straight), :], held.at[way, part, here, :],
                      near_send.at[way, part, target], near_recv.at[way, part, slot], layer, target)

    def spread_copy(way, part, target):
        here = rows_of(me_slab, 0, straight)
        return remote(held.at[way, part, here, :], held.at[way, part, here, :],
                      spread_send.at[way, part, target], near_recv.at[way, part, me_slab], me_layer, target)

    def far_copy(way, part, layer, target, slot):
        return remote(ready.at[way, part, pl.ds(straight, detour), :], passing.at[way, part, slot],
                      far_send.at[way, part, target], far_recv.at[way, part, slot], layer, target)

    def pass_copy(way, part, slot):
        return remote(passing.at[way, part, slot], held.at[way, part, rows_of(slot, straight, detour), :],
                      pass_send.at[way, part, slot], pass_recv.at[way, part, slot], beside(me_layer), me_slab)

    def others():
        return [lax.rem(me_slab + n, slabs) for n in range(1, slabs)]

    def next_layer(way, layer):
        return jnp.where(way == 0, layer + 1, layer - 1)

    def beside(layer):
        return layer + 2 - 4 * ((layer // 2) % 2)

    def same_chip(layer, other):
        return layer // 2 == other // 2

    def send_part(way, part):
        target = next_layer(way, me_layer)

        @pl.when(jnp.logical_and(target >= 0, target < layers))
        def _():
            own_copy(way, part, target).start()
            for other in others():
                far_copy(way, part, beside(target), other, me_slab).start()

            @pl.when(same_chip(me_layer, target))
            def _():
                for other in others():
                    near_copy(way, part, target, other, me_slab).start()

    def put(way, part, value):
        ready[way, part] = value.astype(jnp.bfloat16)
        send_part(way, part)

        @pl.when(way == 0)
        def _():
            down[part] = value

        @pl.when(way == 1)
        def _():
            up[part] = value

    def turn(step, carry):
        pass_way = jnp.where(beside(me_layer) == step, 0, 1)
        pass_here = jnp.logical_or(beside(me_layer) == step, beside(me_layer) == layers - 1 - step)

        @pl.when(jnp.logical_and(step > 0, pass_here))
        def _():
            for part in range(2):
                for slot in others():
                    far_copy(pass_way, part, me_layer, slot, slot).wait_recv()
                    pass_copy(pass_way, part, slot).start()

        way = jnp.where(me_layer == step, 0, 1)
        here = jnp.logical_or(me_layer == step, me_layer == layers - 1 - step)

        @pl.when(jnp.logical_and(step == 0, here))
        def _():
            for part in range(2):
                put(way, part, trace[part])

        @pl.when(jnp.logical_and(step > 0, here))
        def _():
            before = next_layer(1 - way, me_layer)

            for part in range(2):
                own_copy(way, part, me_layer).wait_recv()

                @pl.when(jnp.logical_not(same_chip(before, me_layer)))
                def _():
                    for other in others():
                        spread_copy(way, part, other).start()

            pltpu.make_async_copy(green_down, green.at[way], load_sem.at[way]).wait()
            near = me_slab // (slabs // 2)
            totals = [trace[0], trace[1]]
            for cut in range(2):
                for turn_half in range(2):
                    now = near if turn_half == 0 else 1 - near
                    for n in range(slabs // 2):
                        slot = now * (slabs // 2) + n

                        @pl.when(slot != me_slab)
                        def _():
                            near_copy(way, cut, me_layer, me_slab, slot).wait_recv()
                            pass_copy(way, cut, slot).wait_recv()

                    columns = pl.ds(pl.multiple_of(cut * 2 * half + now * half, 128), half)
                    for part in range(2):
                        totals[part] = totals[part] + jnp.dot(
                            green[way, pl.ds(part * slab, slab), columns],
                            held[way, cut, pl.ds(pl.multiple_of(now * half, 16), half), :],
                            preferred_element_type=jnp.float32,
                        )
                        if cut == 1 and turn_half == 1:
                            put(way, part, totals[part])

        return carry

    lax.fori_loop(0, layers, turn, 0)

    for way in range(2):
        target = next_layer(way, me_layer)
        before = next_layer(1 - way, me_layer)
        is_first = jnp.logical_or(before < 0, before >= layers)
        is_last = jnp.logical_or(target < 0, target >= layers)
        passed = beside(me_layer)
        passed_first = (passed == 0) if way == 0 else (passed == layers - 1)

        @pl.when(is_first)
        def _():
            loads[way].wait()

        for part in range(2):
            @pl.when(jnp.logical_not(is_last))
            def _():
                own_copy(way, part, target).wait_send()
                for other in others():
                    far_copy(way, part, beside(target), other, me_slab).wait_send()

                @pl.when(same_chip(me_layer, target))
                def _():
                    for other in others():
                        near_copy(way, part, target, other, me_slab).wait_send()

            @pl.when(jnp.logical_not(jnp.logical_or(is_first, same_chip(before, me_layer))))
            def _():
                for other in others():
                    spread_copy(way, part, other).wait_send()

            @pl.when(jnp.logical_not(passed_first))
            def _():
                for slot in others():
                    pass_copy(way, part, slot).wait_send()

    for side in range(2):
        @pl.when(sends[side])
        def _():
            for copy in halo_copies(side):
                copy.wait_send()


def local(source, wavenumber, green_down, green_up):
    layers, slabs = lax.axis_size("layer"), lax.axis_size("lat")
    _, parts, slab, lanes = source.shape
    width = slab * slabs
    shape = jax.ShapeDtypeStruct((parts, slab, lanes), jnp.float32)
    vmem = pl.BlockSpec(memory_space=pltpu.VMEM)
    hbm = pl.BlockSpec(memory_space=pltpu.HBM)
    detour = slab * 3 // 8 // 16 * 16
    per_part = pltpu.SemaphoreType.DMA((2, parts))
    per_slab = pltpu.SemaphoreType.DMA((2, parts, slabs))
    down, up = pl.pallas_call(
        functools.partial(kernel, layers, slabs),
        out_shape=(shape, shape),
        in_specs=[hbm] * 4,
        out_specs=(vmem, vmem),
        scratch_shapes=[
            pltpu.VMEM((2, parts * slab, parts * width), jnp.bfloat16),
            pltpu.VMEM((2, parts, width, lanes), jnp.bfloat16),
            pltpu.VMEM((2, parts, slab, lanes), jnp.bfloat16),
            pltpu.VMEM((2, parts, slabs, detour, lanes), jnp.bfloat16),
            pltpu.VMEM((parts, slab, lanes), jnp.float32),
            pltpu.VMEM((parts, slab + 2 * HALO, lanes), jnp.float32),
            pltpu.VMEM((slab + 2 * HALO, lanes), jnp.float32),
            pltpu.SemaphoreType.DMA((4,)),
            pltpu.SemaphoreType.DMA((2, 2)),
            pltpu.SemaphoreType.DMA((2, 2)),
            per_part,
            per_part,
            per_slab,
            per_slab,
            per_slab,
            per_slab,
            per_slab,
            per_slab,
            per_slab,
        ],
        compiler_params=pltpu.CompilerParams(
            collective_id=0, has_side_effects=True, vmem_limit_bytes=32 * 1024 * 1024
        ),
    )(
        source[0],
        wavenumber[0],
        green_down.reshape(parts * slab, parts * width),
        green_up.reshape(parts * slab, parts * width),
    )
    return down[None], up[None]


def solution(mesh):
    return jax.shard_map(
        local,
        mesh=mesh,
        in_specs=(
            P("layer", None, "lat", None),
            P("layer", "lat", None),
            P("layer", None, "lat", None),
            P("layer", None, "lat", None),
        ),
        out_specs=(P("layer", None, "lat", None), P("layer", None, "lat", None)),
        check_vma=False,
    )
```

```python
import functools

import jax
import jax.numpy as jnp
from jax import lax
from jax.experimental import pallas as pl
from jax.experimental.pallas import tpu as pltpu
from jax.sharding import PartitionSpec as P

RELAX = 4
HALO = 8
MESH = pl.DeviceIdType.MESH

relax_weight = 0.8
damping = 0.5


def relaxed(source, wave_sq, inside):
    rows, lanes = wave_sq.shape
    lane = lax.broadcasted_iota(jnp.int32, (rows, lanes), 1)
    first, last = lane == 0, lane == lanes - 1
    diag_real = 4.0 - wave_sq
    diag_imag = damping * wave_sq
    scale = jnp.where(inside, relax_weight, 0.0) / (diag_real * diag_real + diag_imag * diag_imag)
    inverse_real = diag_real * scale
    inverse_imag = -diag_imag * scale

    def beside(field):
        total = pltpu.roll(field, 1, 0) + pltpu.roll(field, rows - 1, 0)
        total = total + jnp.where(first, 0.0, pltpu.roll(field, 1, 1))
        return total + jnp.where(last, 0.0, pltpu.roll(field, lanes - 1, 1))

    real = source[0] * inverse_real - source[1] * inverse_imag
    imag = source[0] * inverse_imag + source[1] * inverse_real
    for _ in range(RELAX - 1):
        res_real = source[0] - (diag_real * real - diag_imag * imag - beside(real))
        res_imag = source[1] - (diag_real * imag + diag_imag * real - beside(imag))
        real = real + res_real * inverse_real - res_imag * inverse_imag
        imag = imag + res_real * inverse_imag + res_imag * inverse_real
    return real, imag


def kernel(layers, slabs, source, wave, green_down, green_up, down, up, green, held, ready, passing, trace, wide_source,
           wide_wave, load_sem, halo_send, halo_recv, own_send, own_recv, near_send, near_recv, spread_send,
           far_send, far_recv, pass_send, pass_recv):
    me_layer, me_slab = lax.axis_index("layer"), lax.axis_index("lat")
    slab = trace.shape[1]
    half = slab * slabs // 2
    detour = passing.shape[2]
    straight = slab - detour
    middle = pl.ds(HALO, slab)

    loads = [
        pltpu.make_async_copy(src, dst, load_sem.at[n])
        for n, (src, dst) in enumerate(
            (
                (green_down, green.at[0]),
                (green_up, green.at[1]),
                (source, wide_source.at[:, middle]),
                (wave, wide_wave.at[middle]),
            )
        )
    ]
    for n in (2, 3, 0, 1):
        loads[n].start()

    barrier = pltpu.get_barrier_semaphore()
    me = me_layer * slabs + me_slab

    def greet(other, carry):
        @pl.when(other != me)
        def _():
            pl.semaphore_signal(barrier, inc=1, device_id=(other // slabs, other % slabs), device_id_type=MESH)

        return carry

    lax.fori_loop(0, layers * slabs, greet, 0)
    pl.semaphore_wait(barrier, layers * slabs - 1)

    def halo_copies(side):
        rows = pl.ds(slab - HALO, HALO) if side == 0 else pl.ds(0, HALO)
        lands = pl.ds(0, HALO) if side == 0 else pl.ds(HALO + slab, HALO)
        other = me_slab + 1 if side == 0 else me_slab - 1
        other = jnp.clip(other, 0, slabs - 1)
        return [
            pltpu.make_async_remote_copy(
                src_ref=src, dst_ref=dst, send_sem=halo_send.at[side, n], recv_sem=halo_recv.at[side, n],
                device_id=(me_layer, other), device_id_type=MESH,
            )
            for n, (src, dst) in enumerate(
                ((source.at[:, rows], wide_source.at[:, lands]), (wave.at[rows], wide_wave.at[lands]))
            )
        ]

    has_next, has_previous = me_slab < slabs - 1, me_slab > 0
    sends, receives = (has_next, has_previous), (has_previous, has_next)
    for side in range(2):
        @pl.when(sends[side])
        def _():
            for copy in halo_copies(side):
                copy.start()

        @pl.when(jnp.logical_not(receives[side]))
        def _():
            lands = pl.ds(0, HALO) if side == 0 else pl.ds(HALO + slab, HALO)
            wide_source[:, lands] = jnp.zeros((2, HALO, source.shape[2]), jnp.float32)
            wide_wave[lands] = jnp.ones((HALO, source.shape[2]), jnp.float32)

    for n in (2, 3):
        loads[n].wait()
    for side in range(2):
        @pl.when(receives[side])
        def _():
            for copy in halo_copies(side):
                copy.wait_recv()

    row = lax.broadcasted_iota(jnp.int32, wide_wave.shape, 0) - HALO + me_slab * slab
    inside = jnp.logical_and(row >= 0, row < slab * slabs)
    field = relaxed(wide_source[...], wide_wave[...], inside)
    for part in range(2):
        trace[part] = field[part][HALO : HALO + slab]

    def remote(src, dst, send, recv, layer, target):
        return pltpu.make_async_remote_copy(
            src_ref=src, dst_ref=dst, send_sem=send, recv_sem=recv,
            device_id=(jnp.clip(layer, 0, layers - 1), target), device_id_type=MESH,
        )

    def rows_of(slot, begin, count):
        return pl.ds(pl.multiple_of(slot * slab + begin, 16), count)

    def own_copy(way, part, layer):
        here = rows_of(me_slab, 0, slab)
        return remote(ready.at[way, part], held.at[way, part, here, :], own_send.at[way, part],
                      own_recv.at[way, part], layer, me_slab)

    def near_copy(way, part, layer, target, slot):
        here = rows_of(slot, 0, straight)
        return remote(ready.at[way, part, pl.ds(0, straight), :], held.at[way, part, here, :],
                      near_send.at[way, part, target], near_recv.at[way, part, slot], layer, target)

    def spread_copy(way, part, target):
        here = rows_of(me_slab, 0, straight)
        return remote(held.at[way, part, here, :], held.at[way, part, here, :],
                      spread_send.at[way, part, target], near_recv.at[way, part, me_slab], me_layer, target)

    def far_copy(way, part, layer):
        return remote(ready.at[way, part, pl.ds(straight, detour), :], passing.at[way, part],
                      far_send.at[way, part], far_recv.at[way, part], layer, me_slab)

    def pass_copy(way, part, target, slot):
        return remote(passing.at[way, part], held.at[way, part, rows_of(slot, straight, detour), :],
                      pass_send.at[way, part, target], pass_recv.at[way, part, slot], beside(me_layer), target)

    def others():
        return [lax.rem(me_slab + n, slabs) for n in range(1, slabs)]

    def next_layer(way, layer):
        return jnp.where(way == 0, layer + 1, layer - 1)

    def beside(layer):
        return layer + 2 - 4 * ((layer // 2) % 2)

    def same_chip(layer, other):
        return layer // 2 == other // 2

    def send_part(way, part):
        target = next_layer(way, me_layer)

        @pl.when(jnp.logical_and(target >= 0, target < layers))
        def _():
            far_copy(way, part, beside(target)).start()
            own_copy(way, part, target).start()

            @pl.when(same_chip(me_layer, target))
            def _():
                for other in others():
                    near_copy(way, part, target, other, me_slab).start()

    def put(way, part, value):
        ready[way, part] = value.astype(jnp.bfloat16)
        send_part(way, part)

        @pl.when(way == 0)
        def _():
            down[part] = value

        @pl.when(way == 1)
        def _():
            up[part] = value

    def turn(step, carry):
        pass_way = jnp.where(beside(me_layer) == step, 0, 1)
        pass_here = jnp.logical_or(beside(me_layer) == step, beside(me_layer) == layers - 1 - step)

        @pl.when(jnp.logical_and(step > 0, pass_here))
        def _():
            for part in range(2):
                far_copy(pass_way, part, me_layer).wait_recv()
                for other in others():
                    pass_copy(pass_way, part, other, me_slab).start()

        way = jnp.where(me_layer == step, 0, 1)
        here = jnp.logical_or(me_layer == step, me_layer == layers - 1 - step)

        @pl.when(jnp.logical_and(step == 0, here))
        def _():
            for part in range(2):
                put(way, part, trace[part])

        @pl.when(jnp.logical_and(step > 0, here))
        def _():
            before = next_layer(1 - way, me_layer)

            for part in range(2):
                own_copy(way, part, me_layer).wait_recv()

                @pl.when(jnp.logical_not(same_chip(before, me_layer)))
                def _():
                    for other in others():
                        spread_copy(way, part, other).start()

            pltpu.make_async_copy(green_down, green.at[way], load_sem.at[way]).wait()
            near = me_slab // (slabs // 2)
            totals = [trace[0], trace[1]]
            for cut in range(2):
                for turn_half in range(2):
                    now = near if turn_half == 0 else 1 - near
                    for n in range(slabs // 2):
                        slot = now * (slabs // 2) + n

                        @pl.when(slot != me_slab)
                        def _():
                            near_copy(way, cut, me_layer, me_slab, slot).wait_recv()
                            pass_copy(way, cut, me_slab, slot).wait_recv()

                    columns = pl.ds(pl.multiple_of(cut * 2 * half + now * half, 128), half)
                    for part in range(2):
                        totals[part] = totals[part] + jnp.dot(
                            green[way, pl.ds(part * slab, slab), columns],
                            held[way, cut, pl.ds(pl.multiple_of(now * half, 16), half), :],
                            preferred_element_type=jnp.float32,
                        )
                        if cut == 1 and turn_half == 1:
                            put(way, part, totals[part])

        return carry

    lax.fori_loop(0, layers, turn, 0)

    for way in range(2):
        target = next_layer(way, me_layer)
        before = next_layer(1 - way, me_layer)
        is_first = jnp.logical_or(before < 0, before >= layers)
        is_last = jnp.logical_or(target < 0, target >= layers)
        passed = beside(me_layer)
        passed_first = (passed == 0) if way == 0 else (passed == layers - 1)

        @pl.when(is_first)
        def _():
            loads[way].wait()

        for part in range(2):
            @pl.when(jnp.logical_not(is_last))
            def _():
                own_copy(way, part, target).wait_send()
                far_copy(way, part, beside(target)).wait_send()

                @pl.when(same_chip(me_layer, target))
                def _():
                    for other in others():
                        near_copy(way, part, target, other, me_slab).wait_send()

            @pl.when(jnp.logical_not(jnp.logical_or(is_first, same_chip(before, me_layer))))
            def _():
                for other in others():
                    spread_copy(way, part, other).wait_send()

            @pl.when(jnp.logical_not(passed_first))
            def _():
                for other in others():
                    pass_copy(way, part, other, me_slab).wait_send()

    for side in range(2):
        @pl.when(sends[side])
        def _():
            for copy in halo_copies(side):
                copy.wait_send()


def local(source, wavenumber, green_down, green_up):
    layers, slabs = lax.axis_size("layer"), lax.axis_size("lat")
    _, parts, slab, lanes = source.shape
    width = slab * slabs
    shape = jax.ShapeDtypeStruct((parts, slab, lanes), jnp.float32)
    vmem = pl.BlockSpec(memory_space=pltpu.VMEM)
    hbm = pl.BlockSpec(memory_space=pltpu.HBM)
    detour = slab * 3 // 8 // 16 * 16
    per_part = pltpu.SemaphoreType.DMA((2, parts))
    per_slab = pltpu.SemaphoreType.DMA((2, parts, slabs))
    down, up = pl.pallas_call(
        functools.partial(kernel, layers, slabs),
        out_shape=(shape, shape),
        in_specs=[hbm] * 4,
        out_specs=(vmem, vmem),
        scratch_shapes=[
            pltpu.VMEM((2, parts * slab, parts * width), jnp.bfloat16),
            pltpu.VMEM((2, parts, width, lanes), jnp.bfloat16),
            pltpu.VMEM((2, parts, slab, lanes), jnp.bfloat16),
            pltpu.VMEM((2, parts, detour, lanes), jnp.bfloat16),
            pltpu.VMEM((parts, slab, lanes), jnp.float32),
            pltpu.VMEM((parts, slab + 2 * HALO, lanes), jnp.float32),
            pltpu.VMEM((slab + 2 * HALO, lanes), jnp.float32),
            pltpu.SemaphoreType.DMA((4,)),
            pltpu.SemaphoreType.DMA((2, 2)),
            pltpu.SemaphoreType.DMA((2, 2)),
            per_part,
            per_part,
            per_slab,
            per_slab,
            per_slab,
            per_part,
            per_part,
            per_slab,
            per_slab,
        ],
        compiler_params=pltpu.CompilerParams(
            collective_id=0, has_side_effects=True, vmem_limit_bytes=60 * 1024 * 1024
        ),
    )(
        source[0],
        wavenumber[0],
        green_down.reshape(parts * slab, parts * width),
        green_up.reshape(parts * slab, parts * width),
    )
    return down[None], up[None]


def solution(mesh):
    return jax.shard_map(
        local,
        mesh=mesh,
        in_specs=(
            P("layer", None, "lat", None),
            P("layer", "lat", None),
            P("layer", None, "lat", None),
            P("layer", None, "lat", None),
        ),
        out_specs=(P("layer", None, "lat", None), P("layer", None, "lat", None)),
        check_vma=False,
    )
```

```python
import functools

import jax
import jax.numpy as jnp
from jax import lax
from jax.experimental import pallas as pl
from jax.experimental.pallas import tpu as pltpu
from jax.sharding import PartitionSpec as P

RELAX = 4
HALO = 8
MESH = pl.DeviceIdType.MESH

relax_weight = 0.8
damping = 0.5


def relaxed(source, wave_sq, inside):
    rows, lanes = wave_sq.shape
    lane = lax.broadcasted_iota(jnp.int32, (rows, lanes), 1)
    first, last = lane == 0, lane == lanes - 1
    diag_real = 4.0 - wave_sq
    diag_imag = damping * wave_sq
    scale = jnp.where(inside, relax_weight, 0.0) / (diag_real * diag_real + diag_imag * diag_imag)
    inverse_real = diag_real * scale
    inverse_imag = -diag_imag * scale

    def beside(field):
        total = pltpu.roll(field, 1, 0) + pltpu.roll(field, rows - 1, 0)
        total = total + jnp.where(first, 0.0, pltpu.roll(field, 1, 1))
        return total + jnp.where(last, 0.0, pltpu.roll(field, lanes - 1, 1))

    real = source[0] * inverse_real - source[1] * inverse_imag
    imag = source[0] * inverse_imag + source[1] * inverse_real
    for _ in range(RELAX - 1):
        res_real = source[0] - (diag_real * real - diag_imag * imag - beside(real))
        res_imag = source[1] - (diag_real * imag + diag_imag * real - beside(imag))
        real = real + res_real * inverse_real - res_imag * inverse_imag
        imag = imag + res_real * inverse_imag + res_imag * inverse_real
    return real, imag


def kernel(layers, slabs, source, wave, green_down, green_up, down, up, green, held, ready, passing, trace, wide_source,
           wide_wave, load_sem, halo_send, halo_recv, own_send, own_recv, spread_send, spread_recv,
           far_send, far_recv, pass_send, pass_recv):
    me_layer, me_slab = lax.axis_index("layer"), lax.axis_index("lat")
    slab = trace.shape[1]
    half = slab * slabs // 2
    detour = passing.shape[3]
    straight = slab - 2 * detour
    middle = pl.ds(HALO, slab)

    loads = [
        pltpu.make_async_copy(src, dst, load_sem.at[n])
        for n, (src, dst) in enumerate(
            (
                (green_down, green.at[0]),
                (green_up, green.at[1]),
                (source, wide_source.at[:, middle]),
                (wave, wide_wave.at[middle]),
            )
        )
    ]
    for n in (2, 3, 0, 1):
        loads[n].start()

    barrier = pltpu.get_barrier_semaphore()
    me = me_layer * slabs + me_slab

    def greet(other, carry):
        @pl.when(other != me)
        def _():
            pl.semaphore_signal(barrier, inc=1, device_id=(other // slabs, other % slabs), device_id_type=MESH)

        return carry

    lax.fori_loop(0, layers * slabs, greet, 0)
    pl.semaphore_wait(barrier, layers * slabs - 1)

    def halo_copies(side):
        rows = pl.ds(slab - HALO, HALO) if side == 0 else pl.ds(0, HALO)
        lands = pl.ds(0, HALO) if side == 0 else pl.ds(HALO + slab, HALO)
        other = me_slab + 1 if side == 0 else me_slab - 1
        other = jnp.clip(other, 0, slabs - 1)
        return [
            pltpu.make_async_remote_copy(
                src_ref=src, dst_ref=dst, send_sem=halo_send.at[side, n], recv_sem=halo_recv.at[side, n],
                device_id=(me_layer, other), device_id_type=MESH,
            )
            for n, (src, dst) in enumerate(
                ((source.at[:, rows], wide_source.at[:, lands]), (wave.at[rows], wide_wave.at[lands]))
            )
        ]

    has_next, has_previous = me_slab < slabs - 1, me_slab > 0
    sends, receives = (has_next, has_previous), (has_previous, has_next)
    for side in range(2):
        @pl.when(sends[side])
        def _():
            for copy in halo_copies(side):
                copy.start()

        @pl.when(jnp.logical_not(receives[side]))
        def _():
            lands = pl.ds(0, HALO) if side == 0 else pl.ds(HALO + slab, HALO)
            wide_source[:, lands] = jnp.zeros((2, HALO, source.shape[2]), jnp.float32)
            wide_wave[lands] = jnp.ones((HALO, source.shape[2]), jnp.float32)

    for n in (2, 3):
        loads[n].wait()
    for side in range(2):
        @pl.when(receives[side])
        def _():
            for copy in halo_copies(side):
                copy.wait_recv()

    row = lax.broadcasted_iota(jnp.int32, wide_wave.shape, 0) - HALO + me_slab * slab
    inside = jnp.logical_and(row >= 0, row < slab * slabs)
    field = relaxed(wide_source[...], wide_wave[...], inside)
    for part in range(2):
        trace[part] = field[part][HALO : HALO + slab]

    def remote(src, dst, send, recv, layer, target):
        return pltpu.make_async_remote_copy(
            src_ref=src, dst_ref=dst, send_sem=send, recv_sem=recv,
            device_id=(jnp.clip(layer, 0, layers - 1), target), device_id_type=MESH,
        )

    def rows_of(slot, begin, count):
        return pl.ds(pl.multiple_of(slot * slab + begin, 16), count)

    def own_copy(way, part, piece, layer):
        begin, count = (0, straight) if piece == 0 else (straight, slab - straight)
        here = rows_of(me_slab, begin, count)
        return remote(ready.at[way, part, pl.ds(begin, count), :], held.at[way, part, here, :],
                      own_send.at[way, part, piece], own_recv.at[way, part, piece], layer, me_slab)

    def spread_copy(way, part, target, slot):
        here = rows_of(slot, 0, straight)
        return remote(held.at[way, part, here, :], held.at[way, part, here, :],
                      spread_send.at[way, part, target], spread_recv.at[way, part, slot], me_layer, target)

    def piece_of(core):
        return pl.ds(pl.multiple_of(straight + core * detour, 16), detour)

    def far_copy(way, part, layer, core):
        return remote(ready.at[way, part, piece_of(core), :], passing.at[way, layer % 2, part],
                      far_send.at[way, part, core], far_recv.at[way, layer % 2, part],
                      helper(layer, core), me_slab)

    def pass_copy(way, part, layer, core, target, slot, direct):
        source_ref = ready.at[way, part, piece_of(core), :] if direct else passing.at[way, layer % 2, part]
        here = rows_of(slot, straight + core * detour, detour)
        return remote(source_ref, held.at[way, part, here, :],
                      pass_send.at[way, layer % 2, part, target], pass_recv.at[way, part, core, slot], layer, target)

    def helper(layer, core):
        chip = layer // 2
        return (chip + 1 - 2 * (chip % 2)) * 2 + core

    def others():
        return [lax.rem(me_slab + n, slabs) for n in range(1, slabs)]

    def next_layer(way, layer):
        return jnp.where(way == 0, layer + 1, layer - 1)

    def send_part(way, part):
        target = next_layer(way, me_layer)

        @pl.when(jnp.logical_and(target >= 0, target < layers))
        def _():
            own_copy(way, part, 0, target).start()
            for core in range(2):
                @pl.when(helper(target, core) != me_layer)
                def _():
                    far_copy(way, part, target, core).start()

                @pl.when(helper(target, core) == me_layer)
                def _():
                    for other in others():
                        pass_copy(way, part, target, core, other, me_slab, True).start()

            own_copy(way, part, 1, target).start()

    def put(way, part, value):
        ready[way, part] = value.astype(jnp.bfloat16)
        send_part(way, part)

        @pl.when(way == 0)
        def _():
            down[part] = value

        @pl.when(way == 1)
        def _():
            up[part] = value

    def turn(step, carry):
        helped = helper(me_layer, 0) // 2
        pass_way = jnp.where(step // 2 == helped, 0, 1)
        pass_here = jnp.logical_or(step // 2 == helped, (layers - 1 - step) // 2 == helped)
        target = jnp.where(pass_way == 0, step, layers - 1 - step)
        pass_here = jnp.logical_and(pass_here, next_layer(1 - pass_way, target) != me_layer)

        @pl.when(jnp.logical_and(step > 0, pass_here))
        def _():
            for part in range(2):
                far_copy(pass_way, part, target, me_layer % 2).wait_recv()
                for other in others():
                    pass_copy(pass_way, part, target, me_layer % 2, other, me_slab, False).start()

        way = jnp.where(me_layer == step, 0, 1)
        here = jnp.logical_or(me_layer == step, me_layer == layers - 1 - step)

        @pl.when(jnp.logical_and(step == 0, here))
        def _():
            for part in range(2):
                put(way, part, trace[part])

        @pl.when(jnp.logical_and(step > 0, here))
        def _():
            for part in range(2):
                own_copy(way, part, 0, me_layer).wait_recv()
                for other in others():
                    spread_copy(way, part, other, me_slab).start()

            pltpu.make_async_copy(green_down, green.at[way], load_sem.at[way]).wait()
            near = me_slab // (slabs // 2)
            totals = [trace[0], trace[1]]
            for cut in range(2):
                own_copy(way, cut, 1, me_layer).wait_recv()
                for turn_half in range(2):
                    now = near if turn_half == 0 else 1 - near
                    for n in range(slabs // 2):
                        slot = now * (slabs // 2) + n

                        @pl.when(slot != me_slab)
                        def _():
                            spread_copy(way, cut, me_slab, slot).wait_recv()
                            for core in range(2):
                                pass_copy(way, cut, me_layer, core, me_slab, slot, False).wait_recv()

                    columns = pl.ds(pl.multiple_of(cut * 2 * half + now * half, 128), half)
                    for part in range(2):
                        totals[part] = totals[part] + jnp.dot(
                            green[way, pl.ds(part * slab, slab), columns],
                            held[way, cut, pl.ds(pl.multiple_of(now * half, 16), half), :],
                            preferred_element_type=jnp.float32,
                        )
                        if cut == 1 and turn_half == 1:
                            put(way, part, totals[part])

        return carry

    lax.fori_loop(0, layers, turn, 0)

    for way in range(2):
        target = next_layer(way, me_layer)
        before = next_layer(1 - way, me_layer)
        is_first = jnp.logical_or(before < 0, before >= layers)
        is_last = jnp.logical_or(target < 0, target >= layers)

        @pl.when(is_first)
        def _():
            loads[way].wait()

        for part in range(2):
            @pl.when(jnp.logical_not(is_last))
            def _():
                for piece in range(2):
                    own_copy(way, part, piece, target).wait_send()
                for core in range(2):
                    @pl.when(helper(target, core) != me_layer)
                    def _():
                        far_copy(way, part, target, core).wait_send()

            @pl.when(jnp.logical_not(is_first))
            def _():
                for other in others():
                    spread_copy(way, part, other, me_slab).wait_send()

            for parity in range(2):
                passed = helper(me_layer, parity)
                passed_first = (passed == 0) if way == 0 else (passed == layers - 1)

                @pl.when(jnp.logical_not(passed_first))
                def _():
                    for other in others():
                        pass_copy(way, part, passed, me_layer % 2, other, me_slab, False).wait_send()

    for side in range(2):
        @pl.when(sends[side])
        def _():
            for copy in halo_copies(side):
                copy.wait_send()


def written(down, up, down_out, up_out, sem):
    copies = [
        pltpu.make_async_copy(src.at[part], dst.at[part], sem.at[way, part])
        for way, (src, dst) in enumerate(((down, down_out), (up, up_out)))
        for part in range(2)
    ]
    for copy in copies:
        copy.start()
    for copy in copies:
        copy.wait()


def local(source, wavenumber, green_down, green_up):
    layers, slabs = lax.axis_size("layer"), lax.axis_size("lat")
    _, parts, slab, lanes = source.shape
    width = slab * slabs
    shape = jax.ShapeDtypeStruct((parts, slab, lanes), jnp.float32)
    vmem = pl.BlockSpec(memory_space=pltpu.VMEM)
    hbm = pl.BlockSpec(memory_space=pltpu.HBM)
    detour = slab // 4 // 16 * 16
    per_piece = pltpu.SemaphoreType.DMA((2, parts, 2))
    per_piece_slab = pltpu.SemaphoreType.DMA((2, 2, parts, slabs))
    per_slab = pltpu.SemaphoreType.DMA((2, parts, slabs))
    down, up = pl.pallas_call(
        functools.partial(kernel, layers, slabs),
        out_shape=(shape, shape),
        in_specs=[hbm] * 4,
        out_specs=(vmem, vmem),
        scratch_shapes=[
            pltpu.VMEM((2, parts * slab, parts * width), jnp.bfloat16),
            pltpu.VMEM((2, parts, width, lanes), jnp.bfloat16),
            pltpu.VMEM((2, parts, slab, lanes), jnp.bfloat16),
            pltpu.VMEM((2, 2, parts, detour, lanes), jnp.bfloat16),
            pltpu.VMEM((parts, slab, lanes), jnp.float32),
            pltpu.VMEM((parts, slab + 2 * HALO, lanes), jnp.float32),
            pltpu.VMEM((slab + 2 * HALO, lanes), jnp.float32),
            pltpu.SemaphoreType.DMA((4,)),
            pltpu.SemaphoreType.DMA((2, 2)),
            pltpu.SemaphoreType.DMA((2, 2)),
            per_piece,
            per_piece,
            per_slab,
            per_slab,
            per_piece,
            per_piece,
            per_piece_slab,
            per_piece_slab,
        ],
        compiler_params=pltpu.CompilerParams(
            collective_id=0, has_side_effects=True, vmem_limit_bytes=60 * 1024 * 1024
        ),
    )(
        source[0],
        wavenumber[0],
        green_down.reshape(parts * slab, parts * width),
        green_up.reshape(parts * slab, parts * width),
    )
    down, up = pl.pallas_call(
        written,
        out_shape=(shape, shape),
        in_specs=[hbm] * 2,
        out_specs=(hbm, hbm),
        scratch_shapes=[pltpu.SemaphoreType.DMA((2, parts))],
        compiler_params=pltpu.CompilerParams(vmem_limit_bytes=60 * 1024 * 1024),
    )(down, up)
    return down[None], up[None]


def solution(mesh):
    return jax.shard_map(
        local,
        mesh=mesh,
        in_specs=(
            P("layer", None, "lat", None),
            P("layer", "lat", None),
            P("layer", None, "lat", None),
            P("layer", None, "lat", None),
        ),
        out_specs=(P("layer", None, "lat", None), P("layer", None, "lat", None)),
        check_vma=False,
    )
```

```python
import functools

import jax
import jax.numpy as jnp
from jax import lax
from jax.experimental import pallas as pl
from jax.experimental.pallas import tpu as pltpu
from jax.sharding import PartitionSpec as P

RELAX = 4
HALO = 8
CHUNKS = 2
MESH = pl.DeviceIdType.MESH

relax_weight = 0.8
damping = 0.5


def relaxed(source, wave_sq, inside):
    rows, lanes = wave_sq.shape
    lane = lax.broadcasted_iota(jnp.int32, (rows, lanes), 1)
    first, last = lane == 0, lane == lanes - 1
    diag_real = 4.0 - wave_sq
    diag_imag = damping * wave_sq
    scale = jnp.where(inside, relax_weight, 0.0) / (diag_real * diag_real + diag_imag * diag_imag)
    inverse_real = diag_real * scale
    inverse_imag = -diag_imag * scale

    def beside(field):
        total = pltpu.roll(field, 1, 0) + pltpu.roll(field, rows - 1, 0)
        total = total + jnp.where(first, 0.0, pltpu.roll(field, 1, 1))
        return total + jnp.where(last, 0.0, pltpu.roll(field, lanes - 1, 1))

    real = source[0] * inverse_real - source[1] * inverse_imag
    imag = source[0] * inverse_imag + source[1] * inverse_real
    for _ in range(RELAX - 1):
        res_real = source[0] - (diag_real * real - diag_imag * imag - beside(real))
        res_imag = source[1] - (diag_real * imag + diag_imag * real - beside(imag))
        real = real + res_real * inverse_real - res_imag * inverse_imag
        imag = imag + res_real * inverse_imag + res_imag * inverse_real
    return real, imag


def kernel(layers, slabs, source, wave, green_down, green_up, down, up, green, held, ready, trace, wide_source,
           wide_wave, load_sem, halo_send, halo_recv, send_sem, recv_sem):
    me_layer, me_slab = lax.axis_index("layer"), lax.axis_index("lat")
    slab = trace.shape[1]
    half = slab * slabs // 2
    lanes = trace.shape[2]
    chunk_lanes = lanes // CHUNKS
    middle = pl.ds(HALO, slab)

    loads = [
        pltpu.make_async_copy(src, dst, load_sem.at[n])
        for n, (src, dst) in enumerate(
            (
                (green_down, green.at[0]),
                (green_up, green.at[1]),
                (source, wide_source.at[:, middle]),
                (wave, wide_wave.at[middle]),
            )
        )
    ]
    for n in (2, 3, 0, 1):
        loads[n].start()

    barrier = pltpu.get_barrier_semaphore()
    me = me_layer * slabs + me_slab

    def greet(other, carry):
        @pl.when(other != me)
        def _():
            pl.semaphore_signal(barrier, inc=1, device_id=(other // slabs, other % slabs), device_id_type=MESH)

        return carry

    lax.fori_loop(0, layers * slabs, greet, 0)
    pl.semaphore_wait(barrier, layers * slabs - 1)

    def halo_copies(side):
        rows = pl.ds(slab - HALO, HALO) if side == 0 else pl.ds(0, HALO)
        lands = pl.ds(0, HALO) if side == 0 else pl.ds(HALO + slab, HALO)
        other = me_slab + 1 if side == 0 else me_slab - 1
        other = jnp.clip(other, 0, slabs - 1)
        return [
            pltpu.make_async_remote_copy(
                src_ref=src, dst_ref=dst, send_sem=halo_send.at[side, n], recv_sem=halo_recv.at[side, n],
                device_id=(me_layer, other), device_id_type=MESH,
            )
            for n, (src, dst) in enumerate(
                ((source.at[:, rows], wide_source.at[:, lands]), (wave.at[rows], wide_wave.at[lands]))
            )
        ]

    has_next, has_previous = me_slab < slabs - 1, me_slab > 0
    sends, receives = (has_next, has_previous), (has_previous, has_next)
    for side in range(2):
        @pl.when(sends[side])
        def _():
            for copy in halo_copies(side):
                copy.start()

        @pl.when(jnp.logical_not(receives[side]))
        def _():
            lands = pl.ds(0, HALO) if side == 0 else pl.ds(HALO + slab, HALO)
            wide_source[:, lands] = jnp.zeros((2, HALO, source.shape[2]), jnp.float32)
            wide_wave[lands] = jnp.ones((HALO, source.shape[2]), jnp.float32)

    for n in (2, 3):
        loads[n].wait()
    for side in range(2):
        @pl.when(receives[side])
        def _():
            for copy in halo_copies(side):
                copy.wait_recv()

    row = lax.broadcasted_iota(jnp.int32, wide_wave.shape, 0) - HALO + me_slab * slab
    inside = jnp.logical_and(row >= 0, row < slab * slabs)
    field = relaxed(wide_source[...], wide_wave[...], inside)
    for part in range(2):
        trace[part] = field[part][HALO : HALO + slab]

    lane = lax.broadcasted_iota(jnp.int32, (slab, lanes), 1)

    def push(way, chunk, target, slot):
        here = pl.ds(pl.multiple_of(slot * slab, 16), slab)
        step = jnp.where(way == 0, 1, -1)
        return pltpu.make_async_remote_copy(
            src_ref=ready.at[way, chunk], dst_ref=held.at[way, chunk, here, :],
            send_sem=send_sem.at[way, chunk, target], recv_sem=recv_sem.at[way, chunk, slot],
            device_id=(jnp.clip(me_layer + step, 0, layers - 1), target), device_id_type=MESH,
        )

    def others_first():
        return [lax.rem(me_slab + n, slabs) for n in range(1, slabs + 1)]

    def put(way, chunk, place, value):
        mine = lane // chunk_lanes == chunk
        packed = jnp.where(mine, value[0], pltpu.roll(value[1], chunk_lanes, 1))
        ready[way, chunk] = packed.astype(jnp.bfloat16)

        @pl.when(place < layers - 1)
        def _():
            if chunk > 0:
                for target in others_first():
                    push(way, chunk - 1, target, me_slab).wait_send()
            for target in others_first():
                push(way, chunk, target, me_slab).start()

        for out, here in ((down, way == 0), (up, way == 1)):
            @pl.when(here)
            def _():
                for part in range(2):
                    out[part] = value[part] if chunk == 0 else jnp.where(mine, value[part], out[part])

    def turn(order, carry):
        way = jnp.where(me_layer < layers // 2, order, 1 - order)
        place = jnp.where(way == 0, me_layer, layers - 1 - me_layer)

        @pl.when(place == 0)
        def _():
            for chunk in range(CHUNKS):
                put(way, chunk, place, (trace[0], trace[1]))

        @pl.when(place > 0)
        def _():
            pltpu.make_async_copy(green_down, green.at[way], load_sem.at[way]).wait()
            near = me_slab // (slabs // 2)
            for chunk in range(CHUNKS):
                totals = [[None, None], [None, None]]
                for turn_half in range(2):
                    now = near if turn_half == 0 else 1 - near
                    for n in range(slabs // 2):
                        push(way, chunk, me_slab, now * (slabs // 2) + n).wait_recv()
                    block = held[way, chunk, pl.ds(pl.multiple_of(now * half, 16), half), :]
                    for part in range(2):
                        for cut in range(2):
                            columns = pl.ds(pl.multiple_of(cut * 2 * half + now * half, 128), half)
                            product = jnp.dot(
                                green[way, pl.ds(part * slab, slab), columns], block,
                                preferred_element_type=jnp.float32,
                            )
                            if turn_half == 0:
                                totals[part][cut] = product
                            else:
                                totals[part][cut] = totals[part][cut] + product
                value = [
                    trace[part] + totals[part][0] + pltpu.roll(totals[part][1], chunk_lanes, 1) for part in range(2)
                ]
                put(way, chunk, place, value)

        return carry

    lax.fori_loop(0, 2, turn, 0)

    for way in range(2):
        place = me_layer if way == 0 else layers - 1 - me_layer

        @pl.when(place == 0)
        def _():
            loads[way].wait()

        @pl.when(place < layers - 1)
        def _():
            for target in others_first():
                push(way, CHUNKS - 1, target, me_slab).wait_send()

    for side in range(2):
        @pl.when(sends[side])
        def _():
            for copy in halo_copies(side):
                copy.wait_send()


def written(down, up, down_out, up_out, held, sem):
    loads = [
        pltpu.make_async_copy(src.at[part], held.at[way, part], sem.at[0, way, part])
        for way, src in enumerate((down, up))
        for part in range(2)
    ]
    stores = [
        pltpu.make_async_copy(held.at[way, part], dst.at[part], sem.at[1, way, part])
        for way, dst in enumerate((down_out, up_out))
        for part in range(2)
    ]
    for load in loads:
        load.start()
    for load, store in zip(loads, stores):
        load.wait()
        store.start()
    for store in stores:
        store.wait()


def local(source, wavenumber, green_down, green_up):
    layers, slabs = lax.axis_size("layer"), lax.axis_size("lat")
    _, parts, slab, lanes = source.shape
    width = slab * slabs
    shape = jax.ShapeDtypeStruct((parts, slab, lanes), jnp.float32)
    vmem = pl.BlockSpec(memory_space=pltpu.VMEM)
    hbm = pl.BlockSpec(memory_space=pltpu.HBM)
    per_slab = pltpu.SemaphoreType.DMA((2, CHUNKS, slabs))
    down, up = pl.pallas_call(
        functools.partial(kernel, layers, slabs),
        out_shape=(shape, shape),
        in_specs=[hbm] * 4,
        out_specs=(vmem, vmem),
        scratch_shapes=[
            pltpu.VMEM((2, parts * slab, parts * width), jnp.bfloat16),
            pltpu.VMEM((2, CHUNKS, width, lanes), jnp.bfloat16),
            pltpu.VMEM((2, CHUNKS, slab, lanes), jnp.bfloat16),
            pltpu.VMEM((parts, slab, lanes), jnp.float32),
            pltpu.VMEM((parts, slab + 2 * HALO, lanes), jnp.float32),
            pltpu.VMEM((slab + 2 * HALO, lanes), jnp.float32),
            pltpu.SemaphoreType.DMA((4,)),
            pltpu.SemaphoreType.DMA((2, 2)),
            pltpu.SemaphoreType.DMA((2, 2)),
            per_slab,
            per_slab,
        ],
        compiler_params=pltpu.CompilerParams(
            collective_id=0, has_side_effects=True, vmem_limit_bytes=60 * 1024 * 1024
        ),
    )(
        source[0],
        wavenumber[0],
        green_down.reshape(parts * slab, parts * width),
        green_up.reshape(parts * slab, parts * width),
    )
    down, up = pl.pallas_call(
        written,
        out_shape=(shape, shape),
        in_specs=[hbm] * 2,
        out_specs=(hbm, hbm),
        scratch_shapes=[
            pltpu.VMEM((2, parts, slab, lanes), jnp.float32),
            pltpu.SemaphoreType.DMA((2, 2, parts)),
        ],
        compiler_params=pltpu.CompilerParams(vmem_limit_bytes=60 * 1024 * 1024),
    )(down, up)
    return down[None], up[None]


def solution(mesh):
    return jax.shard_map(
        local,
        mesh=mesh,
        in_specs=(
            P("layer", None, "lat", None),
            P("layer", "lat", None),
            P("layer", None, "lat", None),
            P("layer", None, "lat", None),
        ),
        out_specs=(P("layer", None, "lat", None), P("layer", None, "lat", None)),
        check_vma=False,
    )
```

```python
import functools

import jax
import jax.numpy as jnp
from jax import lax
from jax.experimental import pallas as pl
from jax.experimental.pallas import tpu as pltpu
from jax.sharding import PartitionSpec as P

RELAX = 4
HALO = 8
CHUNKS = 2
FAR, NEAR = 2, 1
MESH = pl.DeviceIdType.MESH

relax_weight = 0.8
damping = 0.5


def relaxed(source, wave_sq, inside):
    rows, lanes = wave_sq.shape
    lane = lax.broadcasted_iota(jnp.int32, (rows, lanes), 1)
    first, last = lane == 0, lane == lanes - 1
    diag_real = 4.0 - wave_sq
    diag_imag = damping * wave_sq
    scale = jnp.where(inside, relax_weight, 0.0) / (diag_real * diag_real + diag_imag * diag_imag)
    inverse_real = diag_real * scale
    inverse_imag = -diag_imag * scale

    def beside(field):
        total = pltpu.roll(field, 1, 0) + pltpu.roll(field, rows - 1, 0)
        total = total + jnp.where(first, 0.0, pltpu.roll(field, 1, 1))
        return total + jnp.where(last, 0.0, pltpu.roll(field, lanes - 1, 1))

    real = source[0] * inverse_real - source[1] * inverse_imag
    imag = source[0] * inverse_imag + source[1] * inverse_real
    for _ in range(RELAX - 1):
        res_real = source[0] - (diag_real * real - diag_imag * imag - beside(real))
        res_imag = source[1] - (diag_real * imag + diag_imag * real - beside(imag))
        real = real + res_real * inverse_real - res_imag * inverse_imag
        imag = imag + res_real * inverse_imag + res_imag * inverse_real
    return real, imag


def kernel(layers, slabs, source, wave, green_down, green_up, down, up, green, held, ready, trace, wide_source,
           wide_wave, load_sem, halo_send, halo_recv, send_sem, recv_sem, forward_send):
    me_layer, me_slab = lax.axis_index("layer"), lax.axis_index("lat")
    slab = trace.shape[1]
    half = slab * slabs // 2
    lanes = trace.shape[2]
    chunk_lanes = lanes // CHUNKS
    middle = pl.ds(HALO, slab)

    loads = [
        pltpu.make_async_copy(src, dst, load_sem.at[n])
        for n, (src, dst) in enumerate(
            (
                (green_down, green.at[0]),
                (green_up, green.at[1]),
                (source, wide_source.at[:, middle]),
                (wave, wide_wave.at[middle]),
            )
        )
    ]
    for n in (2, 3, 0, 1):
        loads[n].start()

    barrier = pltpu.get_barrier_semaphore()
    me = me_layer * slabs + me_slab

    def greet(other, carry):
        @pl.when(other != me)
        def _():
            pl.semaphore_signal(barrier, inc=1, device_id=(other // slabs, other % slabs), device_id_type=MESH)

        return carry

    lax.fori_loop(0, layers * slabs, greet, 0)
    pl.semaphore_wait(barrier, layers * slabs - 1)

    def halo_copies(side):
        rows = pl.ds(slab - HALO, HALO) if side == 0 else pl.ds(0, HALO)
        lands = pl.ds(0, HALO) if side == 0 else pl.ds(HALO + slab, HALO)
        other = me_slab + 1 if side == 0 else me_slab - 1
        other = jnp.clip(other, 0, slabs - 1)
        return [
            pltpu.make_async_remote_copy(
                src_ref=src, dst_ref=dst, send_sem=halo_send.at[side, n], recv_sem=halo_recv.at[side, n],
                device_id=(me_layer, other), device_id_type=MESH,
            )
            for n, (src, dst) in enumerate(
                ((source.at[:, rows], wide_source.at[:, lands]), (wave.at[rows], wide_wave.at[lands]))
            )
        ]

    has_next, has_previous = me_slab < slabs - 1, me_slab > 0
    sends, receives = (has_next, has_previous), (has_previous, has_next)
    for side in range(2):
        @pl.when(sends[side])
        def _():
            for copy in halo_copies(side):
                copy.start()

        @pl.when(jnp.logical_not(receives[side]))
        def _():
            lands = pl.ds(0, HALO) if side == 0 else pl.ds(HALO + slab, HALO)
            wide_source[:, lands] = jnp.zeros((2, HALO, source.shape[2]), jnp.float32)
            wide_wave[lands] = jnp.ones((HALO, source.shape[2]), jnp.float32)

    for n in (2, 3):
        loads[n].wait()
    for side in range(2):
        @pl.when(receives[side])
        def _():
            for copy in halo_copies(side):
                copy.wait_recv()

    row = lax.broadcasted_iota(jnp.int32, wide_wave.shape, 0) - HALO + me_slab * slab
    inside = jnp.logical_and(row >= 0, row < slab * slabs)
    field = relaxed(wide_source[...], wide_wave[...], inside)
    for part in range(2):
        trace[part] = field[part][HALO : HALO + slab]

    lane = lax.broadcasted_iota(jnp.int32, (slab, lanes), 1)

    def push(way, chunk, target, slot):
        here = pl.ds(pl.multiple_of(slot * slab, 16), slab)
        step = jnp.where(way == 0, 1, -1)
        return pltpu.make_async_remote_copy(
            src_ref=ready.at[way, chunk], dst_ref=held.at[way, chunk, here, :],
            send_sem=send_sem.at[way, chunk, target], recv_sem=recv_sem.at[way, chunk, slot],
            device_id=(jnp.clip(me_layer + step, 0, layers - 1), target), device_id_type=MESH,
        )

    def forward(way, chunk, slot, toward):
        here = pl.ds(pl.multiple_of(jnp.clip(slot, 0, slabs - 1) * slab, 16), slab)
        index = jnp.clip(slot, 0, slabs - 1)
        return pltpu.make_async_remote_copy(
            src_ref=held.at[way, chunk, here, :], dst_ref=held.at[way, chunk, here, :],
            send_sem=forward_send.at[way, chunk, index], recv_sem=recv_sem.at[way, chunk, index],
            device_id=(me_layer, jnp.clip(toward, 0, slabs - 1)), device_id_type=MESH,
        )

    def within(place):
        return jnp.logical_and(place >= 0, place < slabs)

    def reach(layer, other):
        return jnp.where(layer // 2 == other // 2, FAR, NEAR)

    def each_push(way, chunk, act):
        limit = reach(me_layer, jnp.where(way == 0, me_layer + 1, me_layer - 1))
        for distance in range(FAR, -1, -1):
            for sign in (1, -1)[: 1 if distance == 0 else 2]:
                target = me_slab + sign * distance

                @pl.when(jnp.logical_and(within(target), distance <= limit))
                def _():
                    act(push(way, chunk, jnp.clip(target, 0, slabs - 1), me_slab))

    def each_forward(way, chunk, act):
        limit = reach(me_layer, jnp.where(way == 0, me_layer - 1, me_layer + 1))
        for distance in range(1, slabs):
            for sign in (1, -1):
                slot, toward = me_slab - sign * distance, me_slab + sign

                @pl.when(jnp.logical_and(jnp.logical_and(within(slot), within(toward)), distance >= limit))
                def _():
                    act(forward(way, chunk, slot, toward))

    def put(way, chunk, place, value):
        mine = lane // chunk_lanes == chunk
        packed = jnp.where(mine, value[0], pltpu.roll(value[1], chunk_lanes, 1))
        ready[way, chunk] = packed.astype(jnp.bfloat16)

        @pl.when(place < layers - 1)
        def _():
            if chunk > 0:
                each_push(way, chunk - 1, lambda copy: copy.wait_send())
            each_push(way, chunk, lambda copy: copy.start())

        for out, here in ((down, way == 0), (up, way == 1)):
            @pl.when(here)
            def _():
                for part in range(2):
                    out[part] = value[part] if chunk == 0 else jnp.where(mine, value[part], out[part])

    def turn(order, carry):
        way = jnp.where(me_layer < layers // 2, order, 1 - order)
        place = jnp.where(way == 0, me_layer, layers - 1 - me_layer)

        @pl.when(place == 0)
        def _():
            for chunk in range(CHUNKS):
                put(way, chunk, place, (trace[0], trace[1]))

        @pl.when(place > 0)
        def _():
            pltpu.make_async_copy(green_down, green.at[way], load_sem.at[way]).wait()
            near = me_slab // (slabs // 2)
            limit = reach(me_layer, jnp.where(way == 0, me_layer - 1, me_layer + 1))

            def hand_on(copy):
                copy.wait_recv()
                copy.start()

            for chunk in range(CHUNKS):
                each_forward(way, chunk, hand_on)
                totals = [[None, None], [None, None]]
                for turn_half in range(2):
                    now = near if turn_half == 0 else 1 - near
                    for n in range(slabs // 2):
                        slot = now * (slabs // 2) + n
                        toward = jnp.where(slot < me_slab, me_slab + 1, me_slab - 1)
                        handed_on = jnp.logical_and(jnp.where(slot < me_slab, me_slab - slot, slot - me_slab) >= limit, within(toward))

                        @pl.when(jnp.logical_not(handed_on))
                        def _():
                            push(way, chunk, me_slab, slot).wait_recv()

                    block = held[way, chunk, pl.ds(pl.multiple_of(now * half, 16), half), :]
                    for part in range(2):
                        for cut in range(2):
                            columns = pl.ds(pl.multiple_of(cut * 2 * half + now * half, 128), half)
                            product = jnp.dot(
                                green[way, pl.ds(part * slab, slab), columns], block,
                                preferred_element_type=jnp.float32,
                            )
                            if turn_half == 0:
                                totals[part][cut] = product
                            else:
                                totals[part][cut] = totals[part][cut] + product
                value = [
                    trace[part] + totals[part][0] + pltpu.roll(totals[part][1], chunk_lanes, 1) for part in range(2)
                ]
                put(way, chunk, place, value)

        return carry

    lax.fori_loop(0, 2, turn, 0)

    for way in range(2):
        place = me_layer if way == 0 else layers - 1 - me_layer

        @pl.when(place == 0)
        def _():
            loads[way].wait()

        @pl.when(place < layers - 1)
        def _():
            each_push(way, CHUNKS - 1, lambda copy: copy.wait_send())

        @pl.when(place > 0)
        def _():
            for chunk in range(CHUNKS):
                each_forward(way, chunk, lambda copy: copy.wait_send())

    for side in range(2):
        @pl.when(sends[side])
        def _():
            for copy in halo_copies(side):
                copy.wait_send()


def written(down, up, down_out, up_out, held, sem):
    loads = [
        pltpu.make_async_copy(src.at[part], held.at[way, part], sem.at[0, way, part])
        for way, src in enumerate((down, up))
        for part in range(2)
    ]
    stores = [
        pltpu.make_async_copy(held.at[way, part], dst.at[part], sem.at[1, way, part])
        for way, dst in enumerate((down_out, up_out))
        for part in range(2)
    ]
    for load in loads:
        load.start()
    for load, store in zip(loads, stores):
        load.wait()
        store.start()
    for store in stores:
        store.wait()


def local(source, wavenumber, green_down, green_up):
    layers, slabs = lax.axis_size("layer"), lax.axis_size("lat")
    _, parts, slab, lanes = source.shape
    width = slab * slabs
    shape = jax.ShapeDtypeStruct((parts, slab, lanes), jnp.float32)
    vmem = pl.BlockSpec(memory_space=pltpu.VMEM)
    hbm = pl.BlockSpec(memory_space=pltpu.HBM)
    per_slab = pltpu.SemaphoreType.DMA((2, CHUNKS, slabs))
    down, up = pl.pallas_call(
        functools.partial(kernel, layers, slabs),
        out_shape=(shape, shape),
        in_specs=[hbm] * 4,
        out_specs=(vmem, vmem),
        scratch_shapes=[
            pltpu.VMEM((2, parts * slab, parts * width), jnp.bfloat16),
            pltpu.VMEM((2, CHUNKS, width, lanes), jnp.bfloat16),
            pltpu.VMEM((2, CHUNKS, slab, lanes), jnp.bfloat16),
            pltpu.VMEM((parts, slab, lanes), jnp.float32),
            pltpu.VMEM((parts, slab + 2 * HALO, lanes), jnp.float32),
            pltpu.VMEM((slab + 2 * HALO, lanes), jnp.float32),
            pltpu.SemaphoreType.DMA((4,)),
            pltpu.SemaphoreType.DMA((2, 2)),
            pltpu.SemaphoreType.DMA((2, 2)),
            per_slab,
            per_slab,
            per_slab,
        ],
        compiler_params=pltpu.CompilerParams(
            collective_id=0, has_side_effects=True, vmem_limit_bytes=60 * 1024 * 1024
        ),
    )(
        source[0],
        wavenumber[0],
        green_down.reshape(parts * slab, parts * width),
        green_up.reshape(parts * slab, parts * width),
    )
    down, up = pl.pallas_call(
        written,
        out_shape=(shape, shape),
        in_specs=[hbm] * 2,
        out_specs=(hbm, hbm),
        scratch_shapes=[
            pltpu.VMEM((2, parts, slab, lanes), jnp.float32),
            pltpu.SemaphoreType.DMA((2, 2, parts)),
        ],
        compiler_params=pltpu.CompilerParams(vmem_limit_bytes=60 * 1024 * 1024),
    )(down, up)
    return down[None], up[None]


def solution(mesh):
    return jax.shard_map(
        local,
        mesh=mesh,
        in_specs=(
            P("layer", None, "lat", None),
            P("layer", "lat", None),
            P("layer", None, "lat", None),
            P("layer", None, "lat", None),
        ),
        out_specs=(P("layer", None, "lat", None), P("layer", None, "lat", None)),
        check_vma=False,
    )
```

```python
import functools

import jax
import jax.numpy as jnp
from jax import lax
from jax.experimental import pallas as pl
from jax.experimental.pallas import tpu as pltpu
from jax.sharding import PartitionSpec as P

RELAX = 4
HALO = 8
MESH = pl.DeviceIdType.MESH

relax_weight = 0.8
damping = 0.5


def relaxed(source, wave_sq, inside):
    rows, lanes = wave_sq.shape
    lane = lax.broadcasted_iota(jnp.int32, (rows, lanes), 1)
    first, last = lane == 0, lane == lanes - 1
    diag_real = 4.0 - wave_sq
    diag_imag = damping * wave_sq
    scale = jnp.where(inside, relax_weight, 0.0) / (diag_real * diag_real + diag_imag * diag_imag)
    inverse_real = diag_real * scale
    inverse_imag = -diag_imag * scale

    def beside(field):
        total = pltpu.roll(field, 1, 0) + pltpu.roll(field, rows - 1, 0)
        total = total + jnp.where(first, 0.0, pltpu.roll(field, 1, 1))
        return total + jnp.where(last, 0.0, pltpu.roll(field, lanes - 1, 1))

    real = source[0] * inverse_real - source[1] * inverse_imag
    imag = source[0] * inverse_imag + source[1] * inverse_real
    for _ in range(RELAX - 1):
        res_real = source[0] - (diag_real * real - diag_imag * imag - beside(real))
        res_imag = source[1] - (diag_real * imag + diag_imag * real - beside(imag))
        real = real + res_real * inverse_real - res_imag * inverse_imag
        imag = imag + res_real * inverse_imag + res_imag * inverse_real
    return real, imag


def kernel(layers, slabs, source, wave, green_down, green_up, down, up, green, held, ready, passing, trace, wide_source,
           wide_wave, load_sem, halo_send, halo_recv, own_send, own_recv, near_send, near_recv, spread_send,
           far_send, far_recv, pass_send, pass_recv):
    me_layer, me_slab = lax.axis_index("layer"), lax.axis_index("lat")
    slab = trace.shape[1]
    half = slab * slabs // 2
    detour = passing.shape[2]
    straight = slab - detour
    middle = pl.ds(HALO, slab)

    loads = [
        pltpu.make_async_copy(src, dst, load_sem.at[n])
        for n, (src, dst) in enumerate(
            (
                (green_down, green.at[0]),
                (green_up, green.at[1]),
                (source, wide_source.at[:, middle]),
                (wave, wide_wave.at[middle]),
            )
        )
    ]
    for n in (2, 3, 0, 1):
        loads[n].start()

    barrier = pltpu.get_barrier_semaphore()
    me = me_layer * slabs + me_slab

    def greet(other, carry):
        @pl.when(other != me)
        def _():
            pl.semaphore_signal(barrier, inc=1, device_id=(other // slabs, other % slabs), device_id_type=MESH)

        return carry

    lax.fori_loop(0, layers * slabs, greet, 0)
    pl.semaphore_wait(barrier, layers * slabs - 1)

    def halo_copies(side):
        rows = pl.ds(slab - HALO, HALO) if side == 0 else pl.ds(0, HALO)
        lands = pl.ds(0, HALO) if side == 0 else pl.ds(HALO + slab, HALO)
        other = me_slab + 1 if side == 0 else me_slab - 1
        other = jnp.clip(other, 0, slabs - 1)
        return [
            pltpu.make_async_remote_copy(
                src_ref=src, dst_ref=dst, send_sem=halo_send.at[side, n], recv_sem=halo_recv.at[side, n],
                device_id=(me_layer, other), device_id_type=MESH,
            )
            for n, (src, dst) in enumerate(
                ((source.at[:, rows], wide_source.at[:, lands]), (wave.at[rows], wide_wave.at[lands]))
            )
        ]

    has_next, has_previous = me_slab < slabs - 1, me_slab > 0
    sends, receives = (has_next, has_previous), (has_previous, has_next)
    for side in range(2):
        @pl.when(sends[side])
        def _():
            for copy in halo_copies(side):
                copy.start()

        @pl.when(jnp.logical_not(receives[side]))
        def _():
            lands = pl.ds(0, HALO) if side == 0 else pl.ds(HALO + slab, HALO)
            wide_source[:, lands] = jnp.zeros((2, HALO, source.shape[2]), jnp.float32)
            wide_wave[lands] = jnp.ones((HALO, source.shape[2]), jnp.float32)

    for n in (2, 3):
        loads[n].wait()
    for side in range(2):
        @pl.when(receives[side])
        def _():
            for copy in halo_copies(side):
                copy.wait_recv()

    row = lax.broadcasted_iota(jnp.int32, wide_wave.shape, 0) - HALO + me_slab * slab
    inside = jnp.logical_and(row >= 0, row < slab * slabs)
    field = relaxed(wide_source[...], wide_wave[...], inside)
    for part in range(2):
        trace[part] = field[part][HALO : HALO + slab]

    def remote(src, dst, send, recv, layer, target):
        return pltpu.make_async_remote_copy(
            src_ref=src, dst_ref=dst, send_sem=send, recv_sem=recv,
            device_id=(jnp.clip(layer, 0, layers - 1), target), device_id_type=MESH,
        )

    def rows_of(slot, begin, count):
        return pl.ds(pl.multiple_of(slot * slab + begin, 16), count)

    def own_copy(way, part, layer):
        here = rows_of(me_slab, 0, slab)
        return remote(ready.at[way, part], held.at[way, part, here, :], own_send.at[way, part],
                      own_recv.at[way, part], layer, me_slab)

    def near_copy(way, part, layer, target, slot):
        here = rows_of(slot, 0, straight)
        return remote(ready.at[way, part, pl.ds(0, straight), :], held.at[way, part, here, :],
                      near_send.at[way, part, target], near_recv.at[way, part, slot], layer, target)

    def spread_copy(way, part, target):
        here = rows_of(me_slab, 0, straight)
        return remote(held.at[way, part, here, :], held.at[way, part, here, :],
                      spread_send.at[way, part, target], near_recv.at[way, part, me_slab], me_layer, target)

    def far_copy(way, part, layer):
        return remote(ready.at[way, part, pl.ds(straight, detour), :], passing.at[way, part],
                      far_send.at[way, part], far_recv.at[way, part], layer, me_slab)

    def pass_copy(way, part, target, slot):
        return remote(passing.at[way, part], held.at[way, part, rows_of(slot, straight, detour), :],
                      pass_send.at[way, part, target], pass_recv.at[way, part, slot], beside(me_layer), target)

    def others():
        return [lax.rem(me_slab + n, slabs) for n in range(1, slabs)]

    def next_layer(way, layer):
        return jnp.where(way == 0, layer + 1, layer - 1)

    def beside(layer):
        return layer + 2 - 4 * ((layer // 2) % 2)

    def same_chip(layer, other):
        return layer // 2 == other // 2

    def send_part(way, part):
        target = next_layer(way, me_layer)

        @pl.when(jnp.logical_and(target >= 0, target < layers))
        def _():
            far_copy(way, part, beside(target)).start()
            own_copy(way, part, target).start()

            @pl.when(same_chip(me_layer, target))
            def _():
                for other in others():
                    near_copy(way, part, target, other, me_slab).start()

    def put(way, part, value):
        ready[way, part] = value.astype(jnp.bfloat16)
        send_part(way, part)

        @pl.when(way == 0)
        def _():
            down[part] = value

        @pl.when(way == 1)
        def _():
            up[part] = value

    def turn(step, carry):
        pass_way = jnp.where(beside(me_layer) == step, 0, 1)
        pass_here = jnp.logical_or(beside(me_layer) == step, beside(me_layer) == layers - 1 - step)

        @pl.when(jnp.logical_and(step > 0, pass_here))
        def _():
            for part in range(2):
                far_copy(pass_way, part, me_layer).wait_recv()
                for other in others():
                    pass_copy(pass_way, part, other, me_slab).start()

        way = jnp.where(me_layer == step, 0, 1)
        here = jnp.logical_or(me_layer == step, me_layer == layers - 1 - step)

        @pl.when(jnp.logical_and(step == 0, here))
        def _():
            for part in range(2):
                put(way, part, trace[part])

        @pl.when(jnp.logical_and(step > 0, here))
        def _():
            before = next_layer(1 - way, me_layer)

            for part in range(2):
                own_copy(way, part, me_layer).wait_recv()

                @pl.when(jnp.logical_not(same_chip(before, me_layer)))
                def _():
                    for other in others():
                        spread_copy(way, part, other).start()

            pltpu.make_async_copy(green_down, green.at[way], load_sem.at[way]).wait()
            near = me_slab // (slabs // 2)
            totals = [trace[0], trace[1]]
            for cut in range(2):
                for turn_half in range(2):
                    now = near if turn_half == 0 else 1 - near
                    for n in range(slabs // 2):
                        slot = now * (slabs // 2) + n

                        @pl.when(slot != me_slab)
                        def _():
                            near_copy(way, cut, me_layer, me_slab, slot).wait_recv()
                            pass_copy(way, cut, me_slab, slot).wait_recv()

                    columns = pl.ds(pl.multiple_of(cut * 2 * half + now * half, 128), half)
                    for part in range(2):
                        totals[part] = totals[part] + jnp.dot(
                            green[way, pl.ds(part * slab, slab), columns],
                            held[way, cut, pl.ds(pl.multiple_of(now * half, 16), half), :],
                            preferred_element_type=jnp.float32,
                        )
                        if cut == 1 and turn_half == 1:
                            put(way, part, totals[part])

        return carry

    lax.fori_loop(0, layers, turn, 0)

    for way in range(2):
        target = next_layer(way, me_layer)
        before = next_layer(1 - way, me_layer)
        is_first = jnp.logical_or(before < 0, before >= layers)
        is_last = jnp.logical_or(target < 0, target >= layers)
        passed = beside(me_layer)
        passed_first = (passed == 0) if way == 0 else (passed == layers - 1)

        @pl.when(is_first)
        def _():
            loads[way].wait()

        for part in range(2):
            @pl.when(jnp.logical_not(is_last))
            def _():
                own_copy(way, part, target).wait_send()
                far_copy(way, part, beside(target)).wait_send()

                @pl.when(same_chip(me_layer, target))
                def _():
                    for other in others():
                        near_copy(way, part, target, other, me_slab).wait_send()

            @pl.when(jnp.logical_not(jnp.logical_or(is_first, same_chip(before, me_layer))))
            def _():
                for other in others():
                    spread_copy(way, part, other).wait_send()

            @pl.when(jnp.logical_not(passed_first))
            def _():
                for other in others():
                    pass_copy(way, part, other, me_slab).wait_send()

    for side in range(2):
        @pl.when(sends[side])
        def _():
            for copy in halo_copies(side):
                copy.wait_send()


def written(down, up, down_out, up_out, held, sem):
    loads = [
        pltpu.make_async_copy(src.at[part], held.at[way, part], sem.at[0, way, part])
        for way, src in enumerate((down, up))
        for part in range(2)
    ]
    stores = [
        pltpu.make_async_copy(held.at[way, part], dst.at[part], sem.at[1, way, part])
        for way, dst in enumerate((down_out, up_out))
        for part in range(2)
    ]
    for load in loads:
        load.start()
    for load, store in zip(loads, stores):
        load.wait()
        store.start()
    for store in stores:
        store.wait()


def local(source, wavenumber, green_down, green_up):
    layers, slabs = lax.axis_size("layer"), lax.axis_size("lat")
    _, parts, slab, lanes = source.shape
    width = slab * slabs
    shape = jax.ShapeDtypeStruct((parts, slab, lanes), jnp.float32)
    vmem = pl.BlockSpec(memory_space=pltpu.VMEM)
    hbm = pl.BlockSpec(memory_space=pltpu.HBM)
    detour = slab * 3 // 8 // 16 * 16
    per_part = pltpu.SemaphoreType.DMA((2, parts))
    per_slab = pltpu.SemaphoreType.DMA((2, parts, slabs))
    down, up = pl.pallas_call(
        functools.partial(kernel, layers, slabs),
        out_shape=(shape, shape),
        in_specs=[hbm] * 4,
        out_specs=(vmem, vmem),
        scratch_shapes=[
            pltpu.VMEM((2, parts * slab, parts * width), jnp.bfloat16),
            pltpu.VMEM((2, parts, width, lanes), jnp.bfloat16),
            pltpu.VMEM((2, parts, slab, lanes), jnp.bfloat16),
            pltpu.VMEM((2, parts, detour, lanes), jnp.bfloat16),
            pltpu.VMEM((parts, slab, lanes), jnp.float32),
            pltpu.VMEM((parts, slab + 2 * HALO, lanes), jnp.float32),
            pltpu.VMEM((slab + 2 * HALO, lanes), jnp.float32),
            pltpu.SemaphoreType.DMA((4,)),
            pltpu.SemaphoreType.DMA((2, 2)),
            pltpu.SemaphoreType.DMA((2, 2)),
            per_part,
            per_part,
            per_slab,
            per_slab,
            per_slab,
            per_part,
            per_part,
            per_slab,
            per_slab,
        ],
        compiler_params=pltpu.CompilerParams(
            collective_id=0, has_side_effects=True, vmem_limit_bytes=60 * 1024 * 1024
        ),
    )(
        source[0],
        wavenumber[0],
        green_down.reshape(parts * slab, parts * width),
        green_up.reshape(parts * slab, parts * width),
    )
    down, up = pl.pallas_call(
        written,
        out_shape=(shape, shape),
        in_specs=[hbm] * 2,
        out_specs=(hbm, hbm),
        scratch_shapes=[
            pltpu.VMEM((2, parts, slab, lanes), jnp.float32),
            pltpu.SemaphoreType.DMA((2, 2, parts)),
        ],
        compiler_params=pltpu.CompilerParams(vmem_limit_bytes=60 * 1024 * 1024),
    )(down, up)
    return down[None], up[None]


def solution(mesh):
    return jax.shard_map(
        local,
        mesh=mesh,
        in_specs=(
            P("layer", None, "lat", None),
            P("layer", "lat", None),
            P("layer", None, "lat", None),
            P("layer", None, "lat", None),
        ),
        out_specs=(P("layer", None, "lat", None), P("layer", None, "lat", None)),
        check_vma=False,
    )
```

```python
import functools

import jax
import jax.numpy as jnp
from jax import lax
from jax.experimental import pallas as pl
from jax.experimental.pallas import tpu as pltpu
from jax.sharding import PartitionSpec as P

RELAX = 4
HALO = 8
MESH = pl.DeviceIdType.MESH

relax_weight = 0.8
damping = 0.5


def relaxed(source, wave_sq, inside):
    rows, lanes = wave_sq.shape
    lane = lax.broadcasted_iota(jnp.int32, (rows, lanes), 1)
    first, last = lane == 0, lane == lanes - 1
    diag_real = 4.0 - wave_sq
    diag_imag = damping * wave_sq
    scale = jnp.where(inside, relax_weight, 0.0) / (diag_real * diag_real + diag_imag * diag_imag)
    inverse_real = diag_real * scale
    inverse_imag = -diag_imag * scale

    def beside(field):
        total = pltpu.roll(field, 1, 0) + pltpu.roll(field, rows - 1, 0)
        total = total + jnp.where(first, 0.0, pltpu.roll(field, 1, 1))
        return total + jnp.where(last, 0.0, pltpu.roll(field, lanes - 1, 1))

    real = source[0] * inverse_real - source[1] * inverse_imag
    imag = source[0] * inverse_imag + source[1] * inverse_real
    for _ in range(RELAX - 1):
        res_real = source[0] - (diag_real * real - diag_imag * imag - beside(real))
        res_imag = source[1] - (diag_real * imag + diag_imag * real - beside(imag))
        real = real + res_real * inverse_real - res_imag * inverse_imag
        imag = imag + res_real * inverse_imag + res_imag * inverse_real
    return real, imag


def kernel(layers, slabs, source, wave, green_down, green_up, down, up, green, held, ready, passing, trace, wide_source,
           wide_wave, load_sem, halo_send, halo_recv, own_send, own_recv, near_send, near_recv, spread_send,
           far_send, far_recv, pass_send, pass_recv):
    me_layer, me_slab = lax.axis_index("layer"), lax.axis_index("lat")
    slab = trace.shape[1]
    half = slab * slabs // 2
    detour = passing.shape[2]
    straight = slab - detour
    middle = pl.ds(HALO, slab)

    loads = [
        pltpu.make_async_copy(src, dst, load_sem.at[n])
        for n, (src, dst) in enumerate(
            (
                (green_down, green.at[0]),
                (green_up, green.at[1]),
                (source, wide_source.at[:, middle]),
                (wave, wide_wave.at[middle]),
            )
        )
    ]
    for n in (2, 3, 0, 1):
        loads[n].start()

    barrier = pltpu.get_barrier_semaphore()
    me = me_layer * slabs + me_slab

    def greet(other, carry):
        @pl.when(other != me)
        def _():
            pl.semaphore_signal(barrier, inc=1, device_id=(other // slabs, other % slabs), device_id_type=MESH)

        return carry

    lax.fori_loop(0, layers * slabs, greet, 0)
    pl.semaphore_wait(barrier, layers * slabs - 1)

    def halo_copies(side):
        rows = pl.ds(slab - HALO, HALO) if side == 0 else pl.ds(0, HALO)
        lands = pl.ds(0, HALO) if side == 0 else pl.ds(HALO + slab, HALO)
        other = me_slab + 1 if side == 0 else me_slab - 1
        other = jnp.clip(other, 0, slabs - 1)
        return [
            pltpu.make_async_remote_copy(
                src_ref=src, dst_ref=dst, send_sem=halo_send.at[side, n], recv_sem=halo_recv.at[side, n],
                device_id=(me_layer, other), device_id_type=MESH,
            )
            for n, (src, dst) in enumerate(
                ((source.at[:, rows], wide_source.at[:, lands]), (wave.at[rows], wide_wave.at[lands]))
            )
        ]

    has_next, has_previous = me_slab < slabs - 1, me_slab > 0
    sends, receives = (has_next, has_previous), (has_previous, has_next)
    for side in range(2):
        @pl.when(sends[side])
        def _():
            for copy in halo_copies(side):
                copy.start()

        @pl.when(jnp.logical_not(receives[side]))
        def _():
            lands = pl.ds(0, HALO) if side == 0 else pl.ds(HALO + slab, HALO)
            wide_source[:, lands] = jnp.zeros((2, HALO, source.shape[2]), jnp.float32)
            wide_wave[lands] = jnp.ones((HALO, source.shape[2]), jnp.float32)

    for n in (2, 3):
        loads[n].wait()
    for side in range(2):
        @pl.when(receives[side])
        def _():
            for copy in halo_copies(side):
                copy.wait_recv()

    row = lax.broadcasted_iota(jnp.int32, wide_wave.shape, 0) - HALO + me_slab * slab
    inside = jnp.logical_and(row >= 0, row < slab * slabs)
    field = relaxed(wide_source[...], wide_wave[...], inside)
    for part in range(2):
        trace[part] = field[part][HALO : HALO + slab]

    def remote(src, dst, send, recv, layer, target):
        return pltpu.make_async_remote_copy(
            src_ref=src, dst_ref=dst, send_sem=send, recv_sem=recv,
            device_id=(jnp.clip(layer, 0, layers - 1), target), device_id_type=MESH,
        )

    def rows_of(slot, begin, count):
        return pl.ds(pl.multiple_of(slot * slab + begin, 16), count)

    def own_copy(way, part, layer):
        here = rows_of(me_slab, 0, slab)
        return remote(ready.at[way, part], held.at[way, part, here, :], own_send.at[way, part],
                      own_recv.at[way, part], layer, me_slab)

    def near_copy(way, part, layer, target, slot):
        here = rows_of(slot, 0, straight)
        return remote(ready.at[way, part, pl.ds(0, straight), :], held.at[way, part, here, :],
                      near_send.at[way, part, target], near_recv.at[way, part, slot], layer, target)

    def spread_copy(way, part, target):
        here = rows_of(me_slab, 0, straight)
        return remote(held.at[way, part, here, :], held.at[way, part, here, :],
                      spread_send.at[way, part, target], near_recv.at[way, part, me_slab], me_layer, target)

    def far_copy(way, part, layer):
        return remote(ready.at[way, part, pl.ds(straight, detour), :], passing.at[way, part],
                      far_send.at[way, part], far_recv.at[way, part], layer, me_slab)

    def pass_copy(way, part, target, slot):
        return remote(passing.at[way, part], held.at[way, part, rows_of(slot, straight, detour), :],
                      pass_send.at[way, part, target], pass_recv.at[way, part, slot], beside(me_layer), target)

    def others():
        return [lax.rem(me_slab + n, slabs) for n in range(1, slabs)]

    def next_layer(way, layer):
        return jnp.where(way == 0, layer + 1, layer - 1)

    def beside(layer):
        return layer + 2 - 4 * ((layer // 2) % 2)

    def same_chip(layer, other):
        return layer // 2 == other // 2

    def send_part(way, part):
        target = next_layer(way, me_layer)

        @pl.when(jnp.logical_and(target >= 0, target < layers))
        def _():
            far_copy(way, part, beside(target)).start()
            own_copy(way, part, target).start()

            @pl.when(jnp.logical_and(same_chip(me_layer, target), part == 0))
            def _():
                for other in others():
                    near_copy(way, part, target, other, me_slab).start()

    def put(way, part, value):
        ready[way, part] = value.astype(jnp.bfloat16)
        send_part(way, part)

        @pl.when(way == 0)
        def _():
            down[part] = value

        @pl.when(way == 1)
        def _():
            up[part] = value

    def turn(step, carry):
        pass_way = jnp.where(beside(me_layer) == step, 0, 1)
        pass_here = jnp.logical_or(beside(me_layer) == step, beside(me_layer) == layers - 1 - step)

        @pl.when(jnp.logical_and(step > 0, pass_here))
        def _():
            for part in range(2):
                far_copy(pass_way, part, me_layer).wait_recv()
                for other in others():
                    pass_copy(pass_way, part, other, me_slab).start()

        way = jnp.where(me_layer == step, 0, 1)
        here = jnp.logical_or(me_layer == step, me_layer == layers - 1 - step)

        @pl.when(jnp.logical_and(step == 0, here))
        def _():
            for part in range(2):
                put(way, part, trace[part])

        @pl.when(jnp.logical_and(step > 0, here))
        def _():
            before = next_layer(1 - way, me_layer)

            for part in range(2):
                own_copy(way, part, me_layer).wait_recv()

                @pl.when(jnp.logical_or(jnp.logical_not(same_chip(before, me_layer)), part == 1))
                def _():
                    for other in others():
                        spread_copy(way, part, other).start()

            pltpu.make_async_copy(green_down, green.at[way], load_sem.at[way]).wait()
            near = me_slab // (slabs // 2)
            totals = [trace[0], trace[1]]
            for cut in range(2):
                for turn_half in range(2):
                    now = near if turn_half == 0 else 1 - near
                    for n in range(slabs // 2):
                        slot = now * (slabs // 2) + n

                        @pl.when(slot != me_slab)
                        def _():
                            near_copy(way, cut, me_layer, me_slab, slot).wait_recv()
                            pass_copy(way, cut, me_slab, slot).wait_recv()

                    columns = pl.ds(pl.multiple_of(cut * 2 * half + now * half, 128), half)
                    for part in range(2):
                        totals[part] = totals[part] + jnp.dot(
                            green[way, pl.ds(part * slab, slab), columns],
                            held[way, cut, pl.ds(pl.multiple_of(now * half, 16), half), :],
                            preferred_element_type=jnp.float32,
                        )
                        if cut == 1 and turn_half == 1:
                            put(way, part, totals[part])

        return carry

    lax.fori_loop(0, layers, turn, 0)

    for way in range(2):
        target = next_layer(way, me_layer)
        before = next_layer(1 - way, me_layer)
        is_first = jnp.logical_or(before < 0, before >= layers)
        is_last = jnp.logical_or(target < 0, target >= layers)
        passed = beside(me_layer)
        passed_first = (passed == 0) if way == 0 else (passed == layers - 1)

        @pl.when(is_first)
        def _():
            loads[way].wait()

        for part in range(2):
            @pl.when(jnp.logical_not(is_last))
            def _():
                own_copy(way, part, target).wait_send()
                far_copy(way, part, beside(target)).wait_send()

                @pl.when(jnp.logical_and(same_chip(me_layer, target), part == 0))
                def _():
                    for other in others():
                        near_copy(way, part, target, other, me_slab).wait_send()

            spreads = jnp.logical_or(jnp.logical_not(same_chip(before, me_layer)), part == 1)

            @pl.when(jnp.logical_and(jnp.logical_not(is_first), spreads))
            def _():
                for other in others():
                    spread_copy(way, part, other).wait_send()

            @pl.when(jnp.logical_not(passed_first))
            def _():
                for other in others():
                    pass_copy(way, part, other, me_slab).wait_send()

    for side in range(2):
        @pl.when(sends[side])
        def _():
            for copy in halo_copies(side):
                copy.wait_send()


def written(down, up, down_out, up_out, held, sem):
    loads = [
        pltpu.make_async_copy(src.at[part], held.at[way, part], sem.at[0, way, part])
        for way, src in enumerate((down, up))
        for part in range(2)
    ]
    stores = [
        pltpu.make_async_copy(held.at[way, part], dst.at[part], sem.at[1, way, part])
        for way, dst in enumerate((down_out, up_out))
        for part in range(2)
    ]
    for load in loads:
        load.start()
    for load, store in zip(loads, stores):
        load.wait()
        store.start()
    for store in stores:
        store.wait()


def local(source, wavenumber, green_down, green_up):
    layers, slabs = lax.axis_size("layer"), lax.axis_size("lat")
    _, parts, slab, lanes = source.shape
    width = slab * slabs
    shape = jax.ShapeDtypeStruct((parts, slab, lanes), jnp.float32)
    vmem = pl.BlockSpec(memory_space=pltpu.VMEM)
    hbm = pl.BlockSpec(memory_space=pltpu.HBM)
    detour = slab * 3 // 8 // 16 * 16
    per_part = pltpu.SemaphoreType.DMA((2, parts))
    per_slab = pltpu.SemaphoreType.DMA((2, parts, slabs))
    down, up = pl.pallas_call(
        functools.partial(kernel, layers, slabs),
        out_shape=(shape, shape),
        in_specs=[hbm] * 4,
        out_specs=(vmem, vmem),
        scratch_shapes=[
            pltpu.VMEM((2, parts * slab, parts * width), jnp.bfloat16),
            pltpu.VMEM((2, parts, width, lanes), jnp.bfloat16),
            pltpu.VMEM((2, parts, slab, lanes), jnp.bfloat16),
            pltpu.VMEM((2, parts, detour, lanes), jnp.bfloat16),
            pltpu.VMEM((parts, slab, lanes), jnp.float32),
            pltpu.VMEM((parts, slab + 2 * HALO, lanes), jnp.float32),
            pltpu.VMEM((slab + 2 * HALO, lanes), jnp.float32),
            pltpu.SemaphoreType.DMA((4,)),
            pltpu.SemaphoreType.DMA((2, 2)),
            pltpu.SemaphoreType.DMA((2, 2)),
            per_part,
            per_part,
            per_slab,
            per_slab,
            per_slab,
            per_part,
            per_part,
            per_slab,
            per_slab,
        ],
        compiler_params=pltpu.CompilerParams(
            collective_id=0, has_side_effects=True, vmem_limit_bytes=60 * 1024 * 1024
        ),
    )(
        source[0],
        wavenumber[0],
        green_down.reshape(parts * slab, parts * width),
        green_up.reshape(parts * slab, parts * width),
    )
    down, up = pl.pallas_call(
        written,
        out_shape=(shape, shape),
        in_specs=[hbm] * 2,
        out_specs=(hbm, hbm),
        scratch_shapes=[
            pltpu.VMEM((2, parts, slab, lanes), jnp.float32),
            pltpu.SemaphoreType.DMA((2, 2, parts)),
        ],
        compiler_params=pltpu.CompilerParams(vmem_limit_bytes=60 * 1024 * 1024),
    )(down, up)
    return down[None], up[None]


def solution(mesh):
    return jax.shard_map(
        local,
        mesh=mesh,
        in_specs=(
            P("layer", None, "lat", None),
            P("layer", "lat", None),
            P("layer", None, "lat", None),
            P("layer", None, "lat", None),
        ),
        out_specs=(P("layer", None, "lat", None), P("layer", None, "lat", None)),
        check_vma=False,
    )
```

```python
import functools

import jax
import jax.numpy as jnp
from jax import lax
from jax.experimental import pallas as pl
from jax.experimental.pallas import tpu as pltpu
from jax.sharding import PartitionSpec as P

RELAX = 4
HALO = 8
MESH = pl.DeviceIdType.MESH

relax_weight = 0.8
damping = 0.5


def relaxed(source, wave_sq, inside):
    rows, lanes = wave_sq.shape
    lane = lax.broadcasted_iota(jnp.int32, (rows, lanes), 1)
    first, last = lane == 0, lane == lanes - 1
    diag_real = 4.0 - wave_sq
    diag_imag = damping * wave_sq
    scale = jnp.where(inside, relax_weight, 0.0) / (diag_real * diag_real + diag_imag * diag_imag)
    inverse_real = diag_real * scale
    inverse_imag = -diag_imag * scale

    def beside(field):
        total = pltpu.roll(field, 1, 0) + pltpu.roll(field, rows - 1, 0)
        total = total + jnp.where(first, 0.0, pltpu.roll(field, 1, 1))
        return total + jnp.where(last, 0.0, pltpu.roll(field, lanes - 1, 1))

    real = source[0] * inverse_real - source[1] * inverse_imag
    imag = source[0] * inverse_imag + source[1] * inverse_real
    for _ in range(RELAX - 1):
        res_real = source[0] - (diag_real * real - diag_imag * imag - beside(real))
        res_imag = source[1] - (diag_real * imag + diag_imag * real - beside(imag))
        real = real + res_real * inverse_real - res_imag * inverse_imag
        imag = imag + res_real * inverse_imag + res_imag * inverse_real
    return real, imag


def kernel(layers, slabs, source, wave, green_down, green_up, down, up, green, held, ready, passing, trace, wide_source,
           wide_wave, load_sem, halo_send, halo_recv, own_send, own_recv, near_send, near_recv, spread_send,
           far_send, far_recv, pass_send, pass_recv):
    me_layer, me_slab = lax.axis_index("layer"), lax.axis_index("lat")
    slab = trace.shape[1]
    half = slab * slabs // 2
    detour = passing.shape[2]
    straight = slab - detour
    middle = pl.ds(HALO, slab)

    loads = [
        pltpu.make_async_copy(src, dst, load_sem.at[n])
        for n, (src, dst) in enumerate(
            (
                (green_down, green.at[0]),
                (green_up, green.at[1]),
                (source, wide_source.at[:, middle]),
                (wave, wide_wave.at[middle]),
            )
        )
    ]
    for n in (2, 3, 0, 1):
        loads[n].start()

    barrier = pltpu.get_barrier_semaphore()
    me = me_layer * slabs + me_slab

    def greet(other, carry):
        @pl.when(other != me)
        def _():
            pl.semaphore_signal(barrier, inc=1, device_id=(other // slabs, other % slabs), device_id_type=MESH)

        return carry

    lax.fori_loop(0, layers * slabs, greet, 0)
    pl.semaphore_wait(barrier, layers * slabs - 1)

    def halo_copies(side):
        rows = pl.ds(slab - HALO, HALO) if side == 0 else pl.ds(0, HALO)
        lands = pl.ds(0, HALO) if side == 0 else pl.ds(HALO + slab, HALO)
        other = me_slab + 1 if side == 0 else me_slab - 1
        other = jnp.clip(other, 0, slabs - 1)
        return [
            pltpu.make_async_remote_copy(
                src_ref=src, dst_ref=dst, send_sem=halo_send.at[side, n], recv_sem=halo_recv.at[side, n],
                device_id=(me_layer, other), device_id_type=MESH,
            )
            for n, (src, dst) in enumerate(
                ((source.at[:, rows], wide_source.at[:, lands]), (wave.at[rows], wide_wave.at[lands]))
            )
        ]

    has_next, has_previous = me_slab < slabs - 1, me_slab > 0
    sends, receives = (has_next, has_previous), (has_previous, has_next)
    for side in range(2):
        @pl.when(sends[side])
        def _():
            for copy in halo_copies(side):
                copy.start()

        @pl.when(jnp.logical_not(receives[side]))
        def _():
            lands = pl.ds(0, HALO) if side == 0 else pl.ds(HALO + slab, HALO)
            wide_source[:, lands] = jnp.zeros((2, HALO, source.shape[2]), jnp.float32)
            wide_wave[lands] = jnp.ones((HALO, source.shape[2]), jnp.float32)

    for n in (2, 3):
        loads[n].wait()
    for side in range(2):
        @pl.when(receives[side])
        def _():
            for copy in halo_copies(side):
                copy.wait_recv()

    row = lax.broadcasted_iota(jnp.int32, wide_wave.shape, 0) - HALO + me_slab * slab
    inside = jnp.logical_and(row >= 0, row < slab * slabs)
    field = relaxed(wide_source[...], wide_wave[...], inside)
    for part in range(2):
        trace[part] = field[part][HALO : HALO + slab]

    def remote(src, dst, send, recv, layer, target):
        return pltpu.make_async_remote_copy(
            src_ref=src, dst_ref=dst, send_sem=send, recv_sem=recv,
            device_id=(jnp.clip(layer, 0, layers - 1), target), device_id_type=MESH,
        )

    def rows_of(slot, begin, count):
        return pl.ds(pl.multiple_of(slot * slab + begin, 16), count)

    def own_copy(way, part, layer):
        here = rows_of(me_slab, 0, slab)
        return remote(ready.at[way, part], held.at[way, part, here, :], own_send.at[way, part],
                      own_recv.at[way, part], layer, me_slab)

    def near_copy(way, part, layer, target, slot):
        here = rows_of(slot, 0, straight)
        return remote(ready.at[way, part, pl.ds(0, straight), :], held.at[way, part, here, :],
                      near_send.at[way, part, target], near_recv.at[way, part, slot], layer, target)

    def spread_copy(way, part, target):
        here = rows_of(me_slab, 0, straight)
        return remote(held.at[way, part, here, :], held.at[way, part, here, :],
                      spread_send.at[way, part, target], near_recv.at[way, part, me_slab], me_layer, target)

    def far_copy(way, part, layer):
        return remote(ready.at[way, part, pl.ds(straight, detour), :], passing.at[way, part],
                      far_send.at[way, part], far_recv.at[way, part], layer, me_slab)

    def pass_copy(way, part, target, slot):
        return remote(passing.at[way, part], held.at[way, part, rows_of(slot, straight, detour), :],
                      pass_send.at[way, part, target], pass_recv.at[way, part, slot], beside(me_layer), target)

    def others():
        return [lax.rem(me_slab + n, slabs) for n in range(1, slabs)]

    def next_layer(way, layer):
        return jnp.where(way == 0, layer + 1, layer - 1)

    def beside(layer):
        return layer + 2 - 4 * ((layer // 2) % 2)

    def same_chip(layer, other):
        return layer // 2 == other // 2

    def send_part(way, part):
        target = next_layer(way, me_layer)

        @pl.when(jnp.logical_and(target >= 0, target < layers))
        def _():
            far_copy(way, part, beside(target)).start()
            own_copy(way, part, target).start()

            @pl.when(jnp.logical_and(same_chip(me_layer, target), part == 0))
            def _():
                for other in others():
                    near_copy(way, part, target, other, me_slab).start()

    def put(way, part, value):
        ready[way, part] = value.astype(jnp.bfloat16)
        send_part(way, part)

        @pl.when(way == 0)
        def _():
            down[part] = value

        @pl.when(way == 1)
        def _():
            up[part] = value

    def turn(step, carry):
        pass_way = jnp.where(beside(me_layer) == step, 0, 1)
        pass_here = jnp.logical_or(beside(me_layer) == step, beside(me_layer) == layers - 1 - step)

        @pl.when(jnp.logical_and(step > 0, pass_here))
        def _():
            for part in range(2):
                far_copy(pass_way, part, me_layer).wait_recv()
                for other in others():
                    pass_copy(pass_way, part, other, me_slab).start()

        way = jnp.where(me_layer == step, 0, 1)
        here = jnp.logical_or(me_layer == step, me_layer == layers - 1 - step)

        @pl.when(jnp.logical_and(step == 0, here))
        def _():
            for part in range(2):
                put(way, part, trace[part])

        @pl.when(jnp.logical_and(step > 0, here))
        def _():
            before = next_layer(1 - way, me_layer)

            for part in range(2):
                own_copy(way, part, me_layer).wait_recv()

                @pl.when(jnp.logical_or(jnp.logical_not(same_chip(before, me_layer)), part == 1))
                def _():
                    for other in others():
                        spread_copy(way, part, other).start()

            pltpu.make_async_copy(green_down, green.at[way], load_sem.at[way]).wait()
            near = me_slab // (slabs // 2)
            totals = [trace[0], trace[1]]
            for cut in range(2):
                for turn_half in range(2):
                    now = near if turn_half == 0 else 1 - near
                    for n in range(slabs // 2):
                        slot = now * (slabs // 2) + n

                        @pl.when(slot != me_slab)
                        def _():
                            near_copy(way, cut, me_layer, me_slab, slot).wait_recv()
                            pass_copy(way, cut, me_slab, slot).wait_recv()

                    columns = pl.ds(pl.multiple_of(cut * 2 * half + now * half, 128), half)
                    for part in range(2):
                        totals[part] = totals[part] + jnp.dot(
                            green[way, pl.ds(part * slab, slab), columns],
                            held[way, cut, pl.ds(pl.multiple_of(now * half, 16), half), :],
                            preferred_element_type=jnp.float32,
                        )
                        if cut == 1 and turn_half == 1:
                            put(way, part, totals[part])

        return carry

    lax.fori_loop(0, layers, turn, 0)

    for way in range(2):
        target = next_layer(way, me_layer)
        before = next_layer(1 - way, me_layer)
        is_first = jnp.logical_or(before < 0, before >= layers)
        is_last = jnp.logical_or(target < 0, target >= layers)
        passed = beside(me_layer)
        passed_first = (passed == 0) if way == 0 else (passed == layers - 1)

        @pl.when(is_first)
        def _():
            loads[way].wait()

        for part in range(2):
            @pl.when(jnp.logical_not(is_last))
            def _():
                own_copy(way, part, target).wait_send()
                far_copy(way, part, beside(target)).wait_send()

                @pl.when(jnp.logical_and(same_chip(me_layer, target), part == 0))
                def _():
                    for other in others():
                        near_copy(way, part, target, other, me_slab).wait_send()

            spreads = jnp.logical_or(jnp.logical_not(same_chip(before, me_layer)), part == 1)

            @pl.when(jnp.logical_and(jnp.logical_not(is_first), spreads))
            def _():
                for other in others():
                    spread_copy(way, part, other).wait_send()

            @pl.when(jnp.logical_not(passed_first))
            def _():
                for other in others():
                    pass_copy(way, part, other, me_slab).wait_send()

    for side in range(2):
        @pl.when(sends[side])
        def _():
            for copy in halo_copies(side):
                copy.wait_send()


def written(down, up, down_out, up_out, held, sem):
    loads = [
        pltpu.make_async_copy(src.at[part], held.at[way, part], sem.at[0, way, part])
        for way, src in enumerate((down, up))
        for part in range(2)
    ]
    stores = [
        pltpu.make_async_copy(held.at[way, part], dst.at[part], sem.at[1, way, part])
        for way, dst in enumerate((down_out, up_out))
        for part in range(2)
    ]
    for load in loads:
        load.start()
    for load, store in zip(loads, stores):
        load.wait()
        store.start()
    for store in stores:
        store.wait()


def local(source, wavenumber, green_down, green_up):
    layers, slabs = lax.axis_size("layer"), lax.axis_size("lat")
    _, parts, slab, lanes = source.shape
    width = slab * slabs
    shape = jax.ShapeDtypeStruct((parts, slab, lanes), jnp.float32)
    vmem = pl.BlockSpec(memory_space=pltpu.VMEM)
    hbm = pl.BlockSpec(memory_space=pltpu.HBM)
    detour = slab // 4 // 16 * 16
    per_part = pltpu.SemaphoreType.DMA((2, parts))
    per_slab = pltpu.SemaphoreType.DMA((2, parts, slabs))
    down, up = pl.pallas_call(
        functools.partial(kernel, layers, slabs),
        out_shape=(shape, shape),
        in_specs=[hbm] * 4,
        out_specs=(vmem, vmem),
        scratch_shapes=[
            pltpu.VMEM((2, parts * slab, parts * width), jnp.bfloat16),
            pltpu.VMEM((2, parts, width, lanes), jnp.bfloat16),
            pltpu.VMEM((2, parts, slab, lanes), jnp.bfloat16),
            pltpu.VMEM((2, parts, detour, lanes), jnp.bfloat16),
            pltpu.VMEM((parts, slab, lanes), jnp.float32),
            pltpu.VMEM((parts, slab + 2 * HALO, lanes), jnp.float32),
            pltpu.VMEM((slab + 2 * HALO, lanes), jnp.float32),
            pltpu.SemaphoreType.DMA((4,)),
            pltpu.SemaphoreType.DMA((2, 2)),
            pltpu.SemaphoreType.DMA((2, 2)),
            per_part,
            per_part,
            per_slab,
            per_slab,
            per_slab,
            per_part,
            per_part,
            per_slab,
            per_slab,
        ],
        compiler_params=pltpu.CompilerParams(
            collective_id=0, has_side_effects=True, vmem_limit_bytes=60 * 1024 * 1024
        ),
    )(
        source[0],
        wavenumber[0],
        green_down.reshape(parts * slab, parts * width),
        green_up.reshape(parts * slab, parts * width),
    )
    down, up = pl.pallas_call(
        written,
        out_shape=(shape, shape),
        in_specs=[hbm] * 2,
        out_specs=(hbm, hbm),
        scratch_shapes=[
            pltpu.VMEM((2, parts, slab, lanes), jnp.float32),
            pltpu.SemaphoreType.DMA((2, 2, parts)),
        ],
        compiler_params=pltpu.CompilerParams(vmem_limit_bytes=60 * 1024 * 1024),
    )(down, up)
    return down[None], up[None]


def solution(mesh):
    return jax.shard_map(
        local,
        mesh=mesh,
        in_specs=(
            P("layer", None, "lat", None),
            P("layer", "lat", None),
            P("layer", None, "lat", None),
            P("layer", None, "lat", None),
        ),
        out_specs=(P("layer", None, "lat", None), P("layer", None, "lat", None)),
        check_vma=False,
    )
```
